32 devices in a mesh: dp: 8 (over y, x, core), vocab: 4 (over z).
Axes of the slice: x: 2, y: 2, z: 4, core: 2. Of those that a mesh axis runs over, the one named last changes fastest.
Arguments:
- hidden_states: float32 [6144, 2048], P('dp'), may hold values from -8 to 8
- norm_gain: float32 [2048], replicated, may hold values from 0.5 to 1.5
- head_weight: bfloat16 [32768, 2048], P(('vocab', 'dp')), may hold values from -2 to 2
- target_ids: int32 [6144], P('dp'), may hold values from 0 to 32767
- lengths: int32 [8], P('dp'), may hold values from 1 to 768, as said below
Outputs:
- log_probs: float32 [6144], P('dp')
- entropies: float32 [6144], P('dp')
The draws below stay inside these ranges and needn't reach their ends.
Inputs may be any that keep to these rules, and one draw needn't show every extreme that they name: `lengths`: live tokens of a sequence; some sequence fills all 768 slots.
All inputs are finite; a program needn't handle non-finite values.
Results may differ from the reference program's by a relative error of at most 0.0015.
Values may be sent and summed in bfloat16 or wider, within the bound.
A program may use at most 128 MiB of HBM per device.

```python
import jax
import jax.numpy as jnp
from jax import lax

D = 2048
VOCAB = 32768
LEN = 768
SEQS = 8
TOKENS = 6144


def planted_rows(key):
    order = jax.random.permutation(jax.random.fold_in(key, 71), VOCAB)
    chosen_rows = order[:8]
    partner_rows = order[8:16]
    seq_order = jax.random.permutation(jax.random.fold_in(key, 73), SEQS)
    slot_rows = seq_order[:8] * LEN
    signs = jnp.where(jax.random.bernoulli(jax.random.fold_in(key, 74), 0.5, (8, D)), 1.0, -1.0)
    strength = 120.0 + 200.0 * jnp.arange(8, dtype=jnp.float32) / 7.0
    return (chosen_rows, partner_rows, slot_rows, signs, strength)


def draw_head_weight(key, part):
    values = jnp.clip(jax.random.normal(jax.random.fold_in(key, 11), (VOCAB, D), jnp.float32), -6.0, 6.0) * 0.07
    chosen_rows, partner_rows, slot_rows, signs, strength = planted_rows(key)
    values = values.at[chosen_rows].set(signs * (strength[:, None] / D))
    values = values.at[partner_rows].set(signs * ((strength[:, None] - 2.0) / D))
    return values.astype(jnp.bfloat16)


def draw_hidden_states(key, part):
    values = jnp.clip(jax.random.normal(jax.random.fold_in(key, 12), (TOKENS, D), jnp.float32), -6.0, 6.0)
    chosen_rows, partner_rows, slot_rows, signs, strength = planted_rows(key)
    return values.at[slot_rows].set(signs)


def draw_lengths(key, part):
    values = jax.random.randint(jax.random.fold_in(key, 31), (SEQS,), 1, LEN + 1)
    filled = jax.random.randint(jax.random.fold_in(key, 32), (), 0, SEQS)
    return values.at[filled].set(LEN).astype(jnp.int32)


def place_ends(result, own_key, low, high):
    longest = result.shape.index(max(result.shape))
    spots = []
    for shift in (0, 1):
        where = [jax.random.randint(jax.random.fold_in(own_key, axis), (), 0, length) for axis, length in enumerate(result.shape)]
        where[longest] = (where[longest] + shift) % result.shape[longest]
        spots.append(tuple(where))
    return result.at[spots[0]].set(low).at[spots[1]].set(high)


def setup_inputs(seed: int = 0) -> dict:
    key_of = jax.random.split(jax.random.key(seed), 6)
    hidden_states = draw_hidden_states(jax.random.fold_in(key_of[5], 71), 0)
    norm_gain = jnp.clip(1.0 + 0.1 * jax.random.normal(key_of[1], (D,), jnp.float32), 0.5, 1.5)
    head_weight = draw_head_weight(jax.random.fold_in(key_of[5], 71), 0)
    target_ids = place_ends(jax.random.randint(key_of[3], (TOKENS,), 0, VOCAB), jax.random.fold_in(key_of[3], 1), 0, VOCAB - 1).astype(jnp.int32)
    lengths = draw_lengths(jax.random.fold_in(key_of[5], 71), 0)
    return dict(hidden_states=hidden_states, norm_gain=norm_gain, head_weight=head_weight, target_ids=target_ids, lengths=lengths)


epsilon = 1e-05

def reference(hidden_states, norm_gain, head_weight, target_ids, lengths):
    states = hidden_states.reshape(SEQS, LEN, D)
    goals = target_ids.reshape(SEQS, LEN)

    def score_sequence(packed):
        seq_states, seq_goals = packed
        scale = lax.rsqrt(lax.optimization_barrier(jnp.mean(seq_states * seq_states, axis=1, keepdims=True)) + epsilon)
        normed = (seq_states * scale * norm_gain).astype(jnp.bfloat16)
        logits = lax.dot_general(normed, head_weight, (((1,), (1,)), ((), ())), preferred_element_type=jnp.float32)
        maxima = lax.optimization_barrier(jnp.max(logits, axis=1))
        weights = jnp.exp(logits - maxima[:, None])
        totals = lax.optimization_barrier(jnp.sum(weights, axis=1))
        tilted = lax.optimization_barrier(jnp.sum(weights * logits, axis=1))
        log_total = maxima + jnp.log(totals)
        picked = jnp.take_along_axis(logits, seq_goals[:, None].astype(jnp.int32), axis=1)[:, 0]
        return (picked - log_total, log_total - tilted / totals)
    chosen, spread = lax.map(score_sequence, (states, goals))
    positions = jnp.arange(LEN, dtype=jnp.int32)
    live_mask = positions[None, :] < lengths[:, None]
    log_probs = jnp.where(live_mask, chosen, 0.0).reshape(TOKENS)
    entropies = jnp.where(live_mask, spread, 0.0).reshape(TOKENS)
    return (log_probs, entropies)
```

```python
import functools

import jax
import jax.numpy as jnp
from jax import lax
from jax.experimental import pallas as pl
from jax.experimental.pallas import tpu as pltpu
from jax.sharding import PartitionSpec as P

epsilon = 1e-05
lowest = -1e30
MESH = pl.DeviceIdType.MESH
BLOCK = 512


def merge(parts):
    top = parts[0][:, 0:1, :]
    for part in parts[1:]:
        top = jnp.maximum(top, part[:, 0:1, :])
    total = tilted = target = jnp.zeros_like(top)
    for part in parts:
        factor = jnp.exp(part[:, 0:1, :] - top)
        total = total + part[:, 1:2, :] * factor
        tilted = tilted + part[:, 2:3, :] * factor
        target = target + part[:, 3:4, :]
    return top, total, tilted, target


def rows_of(values, shape):
    axis = len(shape) - 2
    row = lax.broadcasted_iota(jnp.int32, shape, axis)
    tile = jnp.zeros(shape, jnp.float32)
    for i, value in enumerate(values):
        tile = jnp.where(row == i, value, tile)
    return tile


def kernel(nz, hid, gain, head, goal, out, T, W, raw, tgt, st, rs, rz,
           hid_sem, w_sem, xs, xr, ys, yr, zs, zr, gs, gr, ss, sr, vs, vr):
    dp = lax.axis_index("dp")
    z = lax.axis_index("vocab")
    core = lax.rem(dp, 2)
    xc = lax.rem(lax.div(dp, 2), 2)
    yc = lax.div(dp, 4)
    p = lax.rem(z, 2)
    q = p + 1
    s = 2 * p
    m = 2 - s
    near_core = (dp + 1 - 2 * core, z)
    near_x = (dp + 2 - 4 * xc, z)
    near_y = (dp + 4 - 8 * yc, z)
    near_d = (dp + 2 - 4 * xc + 4 - 8 * yc, z)
    near_z = (dp, z + 1 - 2 * p)
    far_z = [(dp, lax.rem(z + k, nz)) for k in range(1, nz)]
    partners = [near_core, near_x, near_y, near_d] + far_z

    third = T.shape[2]
    half = third // 2
    entries = head.shape[0]
    base = (z * lax.axis_size("dp") + dp - core) * entries

    def load(t):
        return pltpu.make_async_copy(
            hid.at[pl.ds(t * third, third)], raw.at[t], hid_sem.at[t]
        )

    def send(src, dst, send_sem, recv_sem, where):
        return pltpu.make_async_remote_copy(
            src_ref=src, dst_ref=dst, send_sem=send_sem, recv_sem=recv_sem,
            device_id=where, device_id_type=MESH,
        )

    def piece(slot, t, k):
        return T.at[slot, t, pl.ds((k % 2) * half, half)]

    def X(k):
        if k < 4:
            t = q if k < 2 else p
            return send(piece(0, t, k), piece(1, t, k), xs.at[k], xr.at[k], near_x)
        return send(piece(2, p, k), piece(3, p, k), xs.at[k], xr.at[k], near_x)

    def Y(k):
        if k < 4:
            t = p if k < 2 else q
            return send(piece(0, t, k), piece(2, t, k), ys.at[k], yr.at[k], near_y)
        return send(piece(1, q, k), piece(3, q, k), ys.at[k], yr.at[k], near_y)

    def Z(k):
        slot = (2 - p, 1 + p, 3)[k // 2]
        return send(piece(slot, s, k), piece(slot, s, k), zs.at[k], zr.at[k], near_z)

    def Z_in(k):
        slot = (1 + p, 2 - p, 3)[k // 2]
        return send(piece(slot, m, k), piece(slot, m, k), zs.at[k], zr.at[k], near_z)

    own_rows = pl.ds(core * entries, entries)
    other_rows = pl.ds((1 - core) * entries, entries)
    w_local = pltpu.make_async_copy(head, W.at[own_rows], w_sem.at[0])
    w_send = send(head, W.at[own_rows], w_sem.at[1], w_sem.at[2], near_core)
    w_in = send(head, W.at[other_rows], w_sem.at[1], w_sem.at[2], near_core)
    goals = [
        send(goal, tgt.at[j], gs.at[j - 1], gr.at[j - 1], where)
        for j, where in ((1, near_x), (2, near_y), (3, near_d))
    ]
    stats = [
        send(st.at[j], rs.at[j], ss.at[j - 1], sr.at[j - 1], where)
        for j, where in ((1, near_x), (2, near_y), (3, near_d))
    ]

    for t in (p, q, m):
        load(t).start()
    barrier = pltpu.get_barrier_semaphore()
    for where in partners:
        pl.semaphore_signal(barrier, inc=1, device_id=where, device_id_type=MESH)
    w_local.start()

    def normalise(t):
        load(t).wait()
        states = raw[t]
        scale = lax.rsqrt(jnp.mean(states * states, axis=1, keepdims=True) + epsilon)
        T[0, t] = (states * scale * gain[...]).astype(jnp.bfloat16)

    normalise(p)
    pl.semaphore_wait(barrier, len(partners))
    Y(0).start()
    w_send.start()
    Y(1).start()
    normalise(q)
    X(0).start()
    X(1).start()
    for copy in goals:
        copy.start()
    normalise(m)
    tgt[0] = goal[...]

    def unit(slot, t):
        wanted = tgt[slot, t, 0:1, :] - base

        def body(i, carry):
            top, total, tilted, target = carry
            rows = pl.ds(pl.multiple_of(i * BLOCK, BLOCK), BLOCK)
            logits = lax.dot_general(
                W[rows, :], T[slot, t], (((1,), (1,)), ((), ())),
                preferred_element_type=jnp.float32,
            )
            entry = lax.broadcasted_iota(jnp.int32, logits.shape, 0)
            hit = jnp.where(entry == wanted - i * BLOCK, logits, 0.0)
            target = target + jnp.sum(hit.reshape(BLOCK // 8, 8, third), axis=0)
            logits = logits.reshape(BLOCK // 8, 8, third)
            higher = jnp.maximum(top, jnp.max(logits, axis=0))
            factor = jnp.exp(top - higher)
            weights = jnp.exp(logits - higher[None])
            total = total * factor + jnp.sum(weights, axis=0)
            tilted = tilted * factor + jnp.sum(weights * logits, axis=0)
            return higher, total, tilted, target

        zero = jnp.zeros((8, third), jnp.float32)
        top, total, tilted, target = lax.fori_loop(
            0, W.shape[0] // BLOCK, body, (jnp.full((8, third), lowest, jnp.float32), zero, zero, zero)
        )
        highest = jnp.max(top, axis=0, keepdims=True)
        factor = jnp.exp(top - highest)
        st[slot, t] = rows_of(
            (
                highest,
                jnp.sum(total * factor, axis=0, keepdims=True),
                jnp.sum(tilted * factor, axis=0, keepdims=True),
                jnp.sum(target, axis=0, keepdims=True),
            ),
            (8, third),
        )

    def wave(k):
        X(k).wait_recv()
        Y(k).wait_recv()
        if k < 4:
            X(k + 2).start()
            Y(k + 2).start()
        Z(k).start()

    def units(count, pick):
        def step(u, carry):
            unit(*pick(u))
            return carry

        lax.fori_loop(0, count, step, 0)

    w_local.wait()
    w_in.wait_recv()
    units(2, lambda u: (0, p + u))
    wave(0)
    units(1, lambda u: (0, m))
    for copy in goals:
        copy.wait_recv()
    wave(1)
    units(2, lambda u: (1 + u, q - u))
    wave(2)
    Z_in(0).wait_recv()
    Z_in(1).wait_recv()
    wave(3)
    units(3, lambda u: (jnp.where(u == 2, 1 + p, 1 + u), jnp.where(u == 2, m, p + u)))
    wave(4)
    Z_in(2).wait_recv()
    Z_in(3).wait_recv()
    units(1, lambda u: (2 - p, m))
    stats[0].start()
    stats[1].start()
    wave(5)
    units(2, lambda u: (3, p + u))
    Z_in(4).wait_recv()
    Z_in(5).wait_recv()
    units(1, lambda u: (3, m))
    stats[2].start()
    for copy in stats:
        copy.wait_recv()
    top, total, tilted, target = merge([st[0], rs[1], rs[2], rs[3]])
    rz[z] = rows_of((top, total, tilted, target), (3, 8, third))

    def V(k, source):
        return send(rz.at[source], rz.at[source], vs.at[k - 1], vr.at[k - 1], far_z[k - 1])

    for k in range(1, nz):
        V(k, z).start()
    for k in range(1, nz):
        V(k, lax.rem(z + nz - k, nz)).wait_recv()
    top, total, tilted, target = merge([rz[i] for i in range(nz)])
    log_total = top + jnp.log(total)
    out[...] = rows_of((target - log_total, log_total - tilted / total), (3, 8, third))

    w_send.wait_send()
    for k in range(6):
        X(k).wait_send()
        Y(k).wait_send()
        Z(k).wait_send()
    for copy in goals + stats:
        copy.wait_send()
    for k in range(1, nz):
        V(k, z).wait_send()


def fused(nz, hidden_states, norm_gain, head_weight, target_ids, lengths):
    rows, width = hidden_states.shape
    entries = head_weight.shape[0]
    third = rows // 3
    goal = jnp.broadcast_to(target_ids.reshape(3, 1, third), (3, 8, third))
    dma = pltpu.SemaphoreType.DMA
    any_space = pl.BlockSpec(memory_space=pl.ANY)
    vmem = pl.BlockSpec(memory_space=pltpu.VMEM)
    scores = pl.pallas_call(
        functools.partial(kernel, nz),
        out_shape=jax.ShapeDtypeStruct((3, 8, third), jnp.float32),
        in_specs=[any_space, vmem, any_space, vmem],
        out_specs=vmem,
        scratch_shapes=[
            pltpu.VMEM((4, 3, third, width), jnp.bfloat16),
            pltpu.VMEM((2 * entries, width), jnp.bfloat16),
            pltpu.VMEM((3, third, width), jnp.float32),
            pltpu.VMEM((4, 3, 8, third), jnp.int32),
            pltpu.VMEM((4, 3, 8, third), jnp.float32),
            pltpu.VMEM((4, 3, 8, third), jnp.float32),
            pltpu.VMEM((nz, 3, 8, third), jnp.float32),
            dma((3,)), dma((3,)),
            dma((6,)), dma((6,)), dma((6,)), dma((6,)), dma((6,)), dma((6,)),
            dma((3,)), dma((3,)), dma((3,)), dma((3,)),
            dma((nz - 1,)), dma((nz - 1,)),
        ],
        compiler_params=pltpu.CompilerParams(
            collective_id=0, has_side_effects=True, vmem_limit_bytes=56 * 1024 * 1024
        ),
        cost_estimate=pl.CostEstimate(
            flops=2 * 4 * rows * 2 * entries * width,
            bytes_accessed=rows * width * 4 + entries * width * 2,
            transcendentals=4 * rows * 2 * entries,
        ),
    )(hidden_states, norm_gain.reshape(1, width), head_weight, goal)
    live = jnp.arange(rows, dtype=jnp.int32) < lengths[0]
    log_probs = jnp.where(live, scores[:, 0, :].reshape(rows), 0.0)
    entropies = jnp.where(live, scores[:, 1, :].reshape(rows), 0.0)
    return (log_probs, entropies)


def gathered(hidden_states, norm_gain, head_weight, target_ids, lengths):
    row_count = hidden_states.shape[0]
    scale = lax.rsqrt(jnp.mean(hidden_states * hidden_states, axis=1, keepdims=True) + epsilon)
    normed = (hidden_states * scale * norm_gain).astype(jnp.bfloat16)
    slice_width = head_weight.shape[0] * lax.axis_size("dp")
    goal_cols = target_ids - lax.axis_index("vocab") * slice_width
    live_mask = jnp.arange(row_count, dtype=jnp.int32) < lengths[0]
    logits = lax.dot_general(
        normed, lax.all_gather(head_weight, "dp", axis=0, tiled=True),
        (((1,), (1,)), ((), ())), preferred_element_type=jnp.float32,
    )
    columns = jnp.arange(logits.shape[1], dtype=jnp.int32)
    highest = jnp.max(logits, axis=1)
    weights = jnp.exp(logits - highest[:, None])
    matched = jnp.where(columns[None, :] == goal_cols[:, None], logits, 0.0)
    maxima = lax.pmax(highest, "vocab")
    factor = jnp.exp(highest - maxima)
    totals, tilted, target_logit = lax.psum(
        (
            jnp.sum(weights, axis=1) * factor,
            jnp.sum(weights * logits, axis=1) * factor,
            jnp.sum(matched, axis=1),
        ),
        "vocab",
    )
    log_total = maxima + jnp.log(totals)
    log_probs = jnp.where(live_mask, target_logit - log_total, 0.0)
    entropies = jnp.where(live_mask, log_total - tilted / totals, 0.0)
    return (log_probs, entropies)


def solution(mesh):
    ndp, nz = mesh.shape["dp"], mesh.shape["vocab"]

    def on_device(*args):
        rows, width = args[0].shape
        entries = args[2].shape[0]
        fits = (
            ndp == 8 and nz % 2 == 0 and rows % 768 == 0 and width % 128 == 0
            and 2 * entries % BLOCK == 0
            and 20 * rows * width + 4 * entries * width < 40 * 1024 * 1024
        )
        return fused(nz, *args) if fits else gathered(*args)

    in_specs = (P("dp", None), P(), P(("vocab", "dp"), None), P("dp"), P("dp"))
    out_specs = (P("dp"), P("dp"))
    return jax.shard_map(
        on_device, mesh=mesh, in_specs=in_specs, out_specs=out_specs, check_vma=False
    )
```

```python
import functools

import jax
import jax.numpy as jnp
from jax import lax
from jax.experimental import pallas as pl
from jax.experimental.pallas import tpu as pltpu
from jax.sharding import PartitionSpec as P

epsilon = 1e-05
lowest = -1e30
MESH = pl.DeviceIdType.MESH
BLOCK = 512
PIECES = 4
WINDOW = 2


def merge(parts):
    top = parts[0][:, 0:1, :]
    for part in parts[1:]:
        top = jnp.maximum(top, part[:, 0:1, :])
    total = tilted = target = jnp.zeros_like(top)
    for part in parts:
        factor = jnp.exp(part[:, 0:1, :] - top)
        total = total + part[:, 1:2, :] * factor
        tilted = tilted + part[:, 2:3, :] * factor
        target = target + part[:, 3:4, :]
    return top, total, tilted, target


def rows_of(values, shape):
    axis = len(shape) - 2
    row = lax.broadcasted_iota(jnp.int32, shape, axis)
    tile = jnp.zeros(shape, jnp.float32)
    for i, value in enumerate(values):
        tile = jnp.where(row == i, value, tile)
    return tile


def kernel(nz, hid, gain, head, goal, out, T, W, raw, tgt, acc, st, rs, rz,
           hid_sem, w_sem, xs, xr, ys, yr, zs, zr, gs, gr, ss, sr, vs, vr):
    dp = lax.axis_index("dp")
    z = lax.axis_index("vocab")
    core = lax.rem(dp, 2)
    xc = lax.rem(lax.div(dp, 2), 2)
    yc = lax.div(dp, 4)
    p = lax.rem(z, 2)
    q = p + 1
    s = 2 * p
    m = 2 - s
    near_core = (dp + 1 - 2 * core, z)
    near_x = (dp + 2 - 4 * xc, z)
    near_y = (dp + 4 - 8 * yc, z)
    near_d = (dp + 2 - 4 * xc + 4 - 8 * yc, z)
    near_z = (dp, z + 1 - 2 * p)
    far_z = [(dp, lax.rem(z + k, nz)) for k in range(1, nz)]
    partners = [near_core, near_x, near_y, near_d] + far_z

    third = T.shape[2]
    size = third // PIECES
    waves = 3 * PIECES
    entries = head.shape[0]
    base = (z * lax.axis_size("dp") + dp - core) * entries

    def load(t):
        return pltpu.make_async_copy(
            hid.at[pl.ds(t * third, third)], raw.at[t], hid_sem.at[t]
        )

    def send(src, dst, send_sem, recv_sem, where):
        return pltpu.make_async_remote_copy(
            src_ref=src, dst_ref=dst, send_sem=send_sem, recv_sem=recv_sem,
            device_id=where, device_id_type=MESH,
        )

    def piece(slot, t, k):
        return T.at[slot, t, pl.ds(lax.rem(k, PIECES) * size, size)]

    def X(k):
        g = lax.div(k, PIECES)
        d, t = lax.div(g, 2), q - lax.div(g + 1, 2)
        return send(piece(2 * d, t, k), piece(1 + 2 * d, t, k), xs.at[k], xr.at[k], near_x)

    def Y(k):
        g = lax.div(k, PIECES)
        d, t = lax.div(g, 2), p + lax.div(g + 1, 2)
        return send(piece(d, t, k), piece(2 + d, t, k), ys.at[k], yr.at[k], near_y)

    def Z(k):
        g = lax.div(k, PIECES)
        slot = jnp.where(g == 0, 2 - p, jnp.where(g == 1, 1 + p, 3))
        return send(piece(slot, s, k), piece(slot, s, k), zs.at[k], zr.at[k], near_z)

    def Z_in(k):
        g = lax.div(k, PIECES)
        slot = jnp.where(g == 0, 1 + p, jnp.where(g == 1, 2 - p, 3))
        return send(piece(slot, m, k), piece(slot, m, k), zs.at[k], zr.at[k], near_z)

    own_rows = pl.ds(core * entries, entries)
    other_rows = pl.ds((1 - core) * entries, entries)
    w_local = pltpu.make_async_copy(head, W.at[own_rows], w_sem.at[0])
    w_send = send(head, W.at[own_rows], w_sem.at[1], w_sem.at[2], near_core)
    w_in = send(head, W.at[other_rows], w_sem.at[1], w_sem.at[2], near_core)
    goals = [
        send(goal, tgt.at[j], gs.at[j - 1], gr.at[j - 1], where)
        for j, where in ((1, near_x), (2, near_y), (3, near_d))
    ]
    stats = [
        send(st.at[j], rs.at[j], ss.at[j - 1], sr.at[j - 1], where)
        for j, where in ((1, near_x), (2, near_y), (3, near_d))
    ]

    for t in (p, q, m):
        load(t).start()
    barrier = pltpu.get_barrier_semaphore()
    for where in partners:
        pl.semaphore_signal(barrier, inc=1, device_id=where, device_id_type=MESH)
    w_local.start()

    def normalise(t):
        load(t).wait()
        states = raw[t]
        scale = lax.rsqrt(jnp.mean(states * states, axis=1, keepdims=True) + epsilon)
        T[0, t] = (states * scale * gain[...]).astype(jnp.bfloat16)

    normalise(p)
    pl.semaphore_wait(barrier, len(partners))
    for k in range(WINDOW):
        Y(k).start()
    w_send.start()
    normalise(q)
    for k in range(WINDOW):
        X(k).start()
    for copy in goals:
        copy.start()
    normalise(m)
    tgt[0] = goal[...]
    row = lax.broadcasted_iota(jnp.int32, acc.shape, 2)
    acc[...] = jnp.where(row == 0, lowest, 0.0)
    w_local.wait()
    w_in.wait_recv()

    def block(slot, t, i):
        wanted = tgt[slot, t, 0:1, :] - base
        rows = pl.ds(pl.multiple_of(i * BLOCK, BLOCK), BLOCK)
        logits = lax.dot_general(
            W[rows, :], T[slot, t], (((1,), (1,)), ((), ())),
            preferred_element_type=jnp.float32,
        )
        entry = lax.broadcasted_iota(jnp.int32, logits.shape, 0)
        hit = jnp.where(entry == wanted - i * BLOCK, logits, 0.0)
        logits = logits.reshape(BLOCK // 8, 8, third)
        top = acc[slot, t, 0]
        higher = jnp.maximum(top, jnp.max(logits, axis=0))
        factor = jnp.exp(top - higher)
        weights = jnp.exp(logits - higher[None])
        acc[slot, t, 0] = higher
        acc[slot, t, 1] = acc[slot, t, 1] * factor + jnp.sum(weights, axis=0)
        acc[slot, t, 2] = acc[slot, t, 2] * factor + jnp.sum(weights * logits, axis=0)
        acc[slot, t, 3] = acc[slot, t, 3] + jnp.sum(hit.reshape(BLOCK // 8, 8, third), axis=0)

    blocks = W.shape[0] // BLOCK

    def pick(g, u):
        if g == 0:
            return 0, jnp.where(u == 2, m, p + u)
        if g == 1:
            return jnp.where(u == 2, 1 + p, 1 + u), jnp.where(u == 2, m, q - u)
        if g == 2:
            return jnp.where(u == 2, 2 - p, 1 + u), jnp.where(u == 2, m, p + u)
        return 3, jnp.where(u == 2, m, p + u)

    def work(g, first, count):
        def step(b, carry):
            slot, t = pick(g, lax.div(b, blocks))
            block(slot, t, lax.rem(b, blocks))
            return carry

        lax.fori_loop(first, first + count, step, 0)

    def arrive(g):
        def step(j, carry):
            Z_in(g * PIECES + j).wait_recv()
            return carry

        lax.fori_loop(0, PIECES, step, 0)

    def finish(slot):
        for t in range(3):
            top = acc[slot, t, 0]
            highest = jnp.max(top, axis=0, keepdims=True)
            factor = jnp.exp(top - highest)
            st[slot, t] = rows_of(
                (
                    highest,
                    jnp.sum(acc[slot, t, 1] * factor, axis=0, keepdims=True),
                    jnp.sum(acc[slot, t, 2] * factor, axis=0, keepdims=True),
                    jnp.sum(acc[slot, t, 3], axis=0, keepdims=True),
                ),
                (8, third),
            )

    def wave(k, more):
        X(k).wait_recv()
        Y(k).wait_recv()
        if more:
            X(k + WINDOW).start()
            Y(k + WINDOW).start()
        Z(k).start()

    share = 3 * blocks // PIECES

    def phase(g, first, last, more):
        def step(j, carry):
            wave(g * PIECES + j, more)
            work(g, j * share, share)
            return carry

        lax.fori_loop(first, last, step, 0)

    ready = PIECES // 2
    phase(0, 0, PIECES, True)
    for copy in goals:
        copy.wait_recv()
    phase(1, 0, ready, True)
    arrive(0)
    phase(1, ready, PIECES, True)
    phase(2, 0, ready, True)
    arrive(1)
    phase(2, ready, PIECES, False)
    finish(1)
    finish(2)
    stats[0].start()
    stats[1].start()
    work(3, 0, 2 * blocks)
    finish(0)
    arrive(2)
    work(3, 2 * blocks, blocks)
    finish(3)
    stats[2].start()
    for copy in stats:
        copy.wait_recv()
    top, total, tilted, target = merge([st[0], rs[1], rs[2], rs[3]])
    rz[z] = rows_of((top, total, tilted, target), (3, 8, third))

    def V(k, source):
        return send(rz.at[source], rz.at[source], vs.at[k - 1], vr.at[k - 1], far_z[k - 1])

    for k in range(1, nz):
        V(k, z).start()
    for k in range(1, nz):
        V(k, lax.rem(z + nz - k, nz)).wait_recv()
    top, total, tilted, target = merge([rz[i] for i in range(nz)])
    log_total = top + jnp.log(total)
    out[...] = rows_of((target - log_total, log_total - tilted / total), (3, 8, third))

    w_send.wait_send()

    def sent(k, carry):
        X(k).wait_send()
        Y(k).wait_send()
        Z(k).wait_send()
        return carry

    lax.fori_loop(0, waves, sent, 0)
    for copy in goals + stats:
        copy.wait_send()
    for k in range(1, nz):
        V(k, z).wait_send()


def fused(nz, hidden_states, norm_gain, head_weight, target_ids, lengths):
    rows, width = hidden_states.shape
    entries = head_weight.shape[0]
    third = rows // 3
    goal = jnp.broadcast_to(target_ids.reshape(3, 1, third), (3, 8, third))
    dma = pltpu.SemaphoreType.DMA
    any_space = pl.BlockSpec(memory_space=pl.ANY)
    vmem = pl.BlockSpec(memory_space=pltpu.VMEM)
    scores = pl.pallas_call(
        functools.partial(kernel, nz),
        out_shape=jax.ShapeDtypeStruct((3, 8, third), jnp.float32),
        in_specs=[any_space, vmem, any_space, vmem],
        out_specs=vmem,
        scratch_shapes=[
            pltpu.VMEM((4, 3, third, width), jnp.bfloat16),
            pltpu.VMEM((2 * entries, width), jnp.bfloat16),
            pltpu.VMEM((3, third, width), jnp.float32),
            pltpu.VMEM((4, 3, 8, third), jnp.int32),
            pltpu.VMEM((4, 3, 4, 8, third), jnp.float32),
            pltpu.VMEM((4, 3, 8, third), jnp.float32),
            pltpu.VMEM((4, 3, 8, third), jnp.float32),
            pltpu.VMEM((nz, 3, 8, third), jnp.float32),
            dma((3,)), dma((3,)),
            *[dma((3 * PIECES,)) for _ in range(6)],
            dma((3,)), dma((3,)), dma((3,)), dma((3,)),
            dma((nz - 1,)), dma((nz - 1,)),
        ],
        compiler_params=pltpu.CompilerParams(
            collective_id=0, has_side_effects=True, vmem_limit_bytes=56 * 1024 * 1024
        ),
        cost_estimate=pl.CostEstimate(
            flops=2 * 4 * rows * 2 * entries * width,
            bytes_accessed=rows * width * 4 + entries * width * 2,
            transcendentals=4 * rows * 2 * entries,
        ),
    )(hidden_states, norm_gain.reshape(1, width), head_weight, goal)
    live = jnp.arange(rows, dtype=jnp.int32) < lengths[0]
    log_probs = jnp.where(live, scores[:, 0, :].reshape(rows), 0.0)
    entropies = jnp.where(live, scores[:, 1, :].reshape(rows), 0.0)
    return (log_probs, entropies)


def gathered(hidden_states, norm_gain, head_weight, target_ids, lengths):
    row_count = hidden_states.shape[0]
    scale = lax.rsqrt(jnp.mean(hidden_states * hidden_states, axis=1, keepdims=True) + epsilon)
    normed = (hidden_states * scale * norm_gain).astype(jnp.bfloat16)
    slice_width = head_weight.shape[0] * lax.axis_size("dp")
    goal_cols = target_ids - lax.axis_index("vocab") * slice_width
    live_mask = jnp.arange(row_count, dtype=jnp.int32) < lengths[0]
    logits = lax.dot_general(
        normed, lax.all_gather(head_weight, "dp", axis=0, tiled=True),
        (((1,), (1,)), ((), ())), preferred_element_type=jnp.float32,
    )
    columns = jnp.arange(logits.shape[1], dtype=jnp.int32)
    highest = jnp.max(logits, axis=1)
    weights = jnp.exp(logits - highest[:, None])
    matched = jnp.where(columns[None, :] == goal_cols[:, None], logits, 0.0)
    maxima = lax.pmax(highest, "vocab")
    factor = jnp.exp(highest - maxima)
    totals, tilted, target_logit = lax.psum(
        (
            jnp.sum(weights, axis=1) * factor,
            jnp.sum(weights * logits, axis=1) * factor,
            jnp.sum(matched, axis=1),
        ),
        "vocab",
    )
    log_total = maxima + jnp.log(totals)
    log_probs = jnp.where(live_mask, target_logit - log_total, 0.0)
    entropies = jnp.where(live_mask, log_total - tilted / totals, 0.0)
    return (log_probs, entropies)


def solution(mesh):
    ndp, nz = mesh.shape["dp"], mesh.shape["vocab"]

    def on_device(*args):
        rows, width = args[0].shape
        entries = args[2].shape[0]
        fits = (
            ndp == 8 and nz % 2 == 0 and rows % 768 == 0 and width % 128 == 0
            and 2 * entries % BLOCK == 0
            and 20 * rows * width + 4 * entries * width < 40 * 1024 * 1024
        )
        return fused(nz, *args) if fits else gathered(*args)

    in_specs = (P("dp", None), P(), P(("vocab", "dp"), None), P("dp"), P("dp"))
    out_specs = (P("dp"), P("dp"))
    return jax.shard_map(
        on_device, mesh=mesh, in_specs=in_specs, out_specs=out_specs, check_vma=False
    )
```

```python
import functools

import jax
import jax.numpy as jnp
from jax import lax
from jax.experimental import pallas as pl
from jax.experimental.pallas import tpu as pltpu
from jax.sharding import PartitionSpec as P

epsilon = 1e-05
lowest = -1e30
MESH = pl.DeviceIdType.MESH
BLOCK = 512
PIECES = 4
WINDOW = 2


def merge(parts):
    top = parts[0][:, 0:1, :]
    for part in parts[1:]:
        top = jnp.maximum(top, part[:, 0:1, :])
    total = tilted = target = jnp.zeros_like(top)
    for part in parts:
        factor = jnp.exp(part[:, 0:1, :] - top)
        total = total + part[:, 1:2, :] * factor
        tilted = tilted + part[:, 2:3, :] * factor
        target = target + part[:, 3:4, :]
    return top, total, tilted, target


def rows_of(values, shape):
    axis = len(shape) - 2
    row = lax.broadcasted_iota(jnp.int32, shape, axis)
    tile = jnp.zeros(shape, jnp.float32)
    for i, value in enumerate(values):
        tile = jnp.where(row == i, value, tile)
    return tile


def kernel(nz, hid, gain, head, goal, out, T, W, raw, tgt, st, rs, rz,
           hid_sem, w_sem, xs, xr, ys, yr, zs, zr, gs, gr, ss, sr, vs, vr):
    dp = lax.axis_index("dp")
    z = lax.axis_index("vocab")
    core = lax.rem(dp, 2)
    xc = lax.rem(lax.div(dp, 2), 2)
    yc = lax.div(dp, 4)
    p = lax.rem(z, 2)
    q = p + 1
    s = 2 * p
    m = 2 - s
    near_core = (dp + 1 - 2 * core, z)
    near_x = (dp + 2 - 4 * xc, z)
    near_y = (dp + 4 - 8 * yc, z)
    near_d = (dp + 2 - 4 * xc + 4 - 8 * yc, z)
    near_z = (dp, z + 1 - 2 * p)
    far_z = [(dp, lax.rem(z + k, nz)) for k in range(1, nz)]
    partners = [near_core, near_x, near_y, near_d] + far_z

    width, third = T.shape[2:]
    size = width // PIECES
    waves = 3 * PIECES
    entries = head.shape[0]
    base = (z * lax.axis_size("dp") + dp - core) * entries

    def load(t):
        return pltpu.make_async_copy(
            hid.at[pl.ds(t * third, third)], raw.at[t], hid_sem.at[t]
        )

    def send(src, dst, send_sem, recv_sem, where):
        return pltpu.make_async_remote_copy(
            src_ref=src, dst_ref=dst, send_sem=send_sem, recv_sem=recv_sem,
            device_id=where, device_id_type=MESH,
        )

    def piece(slot, t, k):
        return T.at[slot, t, pl.ds(lax.rem(k, PIECES) * size, size)]

    def X(k):
        g = lax.div(k, PIECES)
        d, t = lax.div(g, 2), q - lax.div(g + 1, 2)
        return send(piece(2 * d, t, k), piece(1 + 2 * d, t, k), xs.at[k], xr.at[k], near_x)

    def Y(k):
        g = lax.div(k, PIECES)
        d, t = lax.div(g, 2), p + lax.div(g + 1, 2)
        return send(piece(d, t, k), piece(2 + d, t, k), ys.at[k], yr.at[k], near_y)

    def Z(k):
        g = lax.div(k, PIECES)
        slot = jnp.where(g == 0, 2 - p, jnp.where(g == 1, 1 + p, 3))
        return send(piece(slot, s, k), piece(slot, s, k), zs.at[k], zr.at[k], near_z)

    def Z_in(k):
        g = lax.div(k, PIECES)
        slot = jnp.where(g == 0, 1 + p, jnp.where(g == 1, 2 - p, 3))
        return send(piece(slot, m, k), piece(slot, m, k), zs.at[k], zr.at[k], near_z)

    own_rows = pl.ds(core * entries, entries)
    other_rows = pl.ds((1 - core) * entries, entries)
    w_local = pltpu.make_async_copy(head, W.at[own_rows], w_sem.at[0])
    w_send = send(head, W.at[own_rows], w_sem.at[1], w_sem.at[2], near_core)
    w_in = send(head, W.at[other_rows], w_sem.at[1], w_sem.at[2], near_core)
    goals = [
        send(goal, tgt.at[j], gs.at[j - 1], gr.at[j - 1], where)
        for j, where in ((1, near_x), (2, near_y), (3, near_d))
    ]
    stats = [
        send(st.at[j], rs.at[j], ss.at[j - 1], sr.at[j - 1], where)
        for j, where in ((1, near_x), (2, near_y), (3, near_d))
    ]

    for t in (p, q, m):
        load(t).start()
    barrier = pltpu.get_barrier_semaphore()
    for where in partners:
        pl.semaphore_signal(barrier, inc=1, device_id=where, device_id_type=MESH)
    w_local.start()

    def normalise(t):
        load(t).wait()
        states = raw[t]
        scale = lax.rsqrt(jnp.mean(states * states, axis=1, keepdims=True) + epsilon)
        T[0, t] = (states * scale * gain[...]).astype(jnp.bfloat16).T

    normalise(p)
    pl.semaphore_wait(barrier, len(partners))
    for k in range(WINDOW):
        Y(k).start()
    w_send.start()
    normalise(q)
    for k in range(WINDOW):
        X(k).start()
    for copy in goals:
        copy.start()
    normalise(m)
    tgt[0] = goal[...]
    w_local.wait()
    w_in.wait_recv()

    def unit(slot, t):
        wanted = tgt[slot, t, 0:1, :] - base
        zero = jnp.zeros((8, third), jnp.float32)
        top, total, tilted, target = jnp.full((8, third), lowest, jnp.float32), zero, zero, zero
        for i in range(W.shape[0] // BLOCK):
            logits = jnp.dot(
                W[pl.ds(i * BLOCK, BLOCK), :], T[slot, t], preferred_element_type=jnp.float32
            )
            entry = lax.broadcasted_iota(jnp.int32, logits.shape, 0)
            hit = jnp.where(entry == wanted - i * BLOCK, logits, 0.0)
            target = target + jnp.sum(hit.reshape(BLOCK // 8, 8, third), axis=0)
            logits = logits.reshape(BLOCK // 8, 8, third)
            higher = jnp.maximum(top, jnp.max(logits, axis=0))
            factor = jnp.exp(top - higher)
            weights = jnp.exp(logits - higher[None])
            total = total * factor + jnp.sum(weights, axis=0)
            tilted = tilted * factor + jnp.sum(weights * logits, axis=0)
            top = higher
        highest = jnp.max(top, axis=0, keepdims=True)
        factor = jnp.exp(top - highest)
        st[slot, t] = rows_of(
            (
                highest,
                jnp.sum(total * factor, axis=0, keepdims=True),
                jnp.sum(tilted * factor, axis=0, keepdims=True),
                jnp.sum(target, axis=0, keepdims=True),
            ),
            (8, third),
        )

    def pick(g, u):
        slot = jnp.where(g == 0, 0, jnp.where(g == 3, 3, 1 + u))
        t = jnp.where(g == 1, q - u, p + u)
        late = jnp.where(g == 1, 1 + p, jnp.where(g == 2, 2 - p, g))
        return jnp.where(u == 2, late, slot), jnp.where(u == 2, m, t)

    def step(k, carry):
        g, j = lax.div(k, PIECES), lax.rem(k, PIECES)

        @pl.when(k < waves)
        def _():
            X(k).wait_recv()
            Y(k).wait_recv()
            Z(k).start()

        @pl.when(k + WINDOW < waves)
        def _():
            X(k + WINDOW).start()
            Y(k + WINDOW).start()

        @pl.when(k == PIECES)
        def _():
            for copy in goals:
                copy.wait_recv()

        @pl.when(k == waves)
        def _():
            stats[0].start()
            stats[1].start()

        @pl.when((j == 2) & (g > 0))
        def _():
            def arrive(i, carry):
                Z_in((g - 1) * PIECES + i).wait_recv()
                return carry

            lax.fori_loop(0, PIECES, arrive, 0)

        @pl.when(j < 3)
        def _():
            unit(*pick(g, j))

        return carry

    lax.fori_loop(0, waves + 3, step, 0)
    stats[2].start()
    for copy in stats:
        copy.wait_recv()
    top, total, tilted, target = merge([st[0], rs[1], rs[2], rs[3]])
    rz[z] = rows_of((top, total, tilted, target), (3, 8, third))

    def V(k, source):
        return send(rz.at[source], rz.at[source], vs.at[k - 1], vr.at[k - 1], far_z[k - 1])

    for k in range(1, nz):
        V(k, z).start()
    for k in range(1, nz):
        V(k, lax.rem(z + nz - k, nz)).wait_recv()
    top, total, tilted, target = merge([rz[i] for i in range(nz)])
    log_total = top + jnp.log(total)
    out[...] = rows_of((target - log_total, log_total - tilted / total), (3, 8, third))

    w_send.wait_send()

    def sent(k, carry):
        X(k).wait_send()
        Y(k).wait_send()
        Z(k).wait_send()
        return carry

    lax.fori_loop(0, waves, sent, 0)
    for copy in goals + stats:
        copy.wait_send()
    for k in range(1, nz):
        V(k, z).wait_send()


def fused(nz, hidden_states, norm_gain, head_weight, target_ids, lengths):
    rows, width = hidden_states.shape
    entries = head_weight.shape[0]
    third = rows // 3
    goal = jnp.broadcast_to(target_ids.reshape(3, 1, third), (3, 8, third))
    dma = pltpu.SemaphoreType.DMA
    any_space = pl.BlockSpec(memory_space=pl.ANY)
    vmem = pl.BlockSpec(memory_space=pltpu.VMEM)
    scores = pl.pallas_call(
        functools.partial(kernel, nz),
        out_shape=jax.ShapeDtypeStruct((3, 8, third), jnp.float32),
        in_specs=[any_space, vmem, any_space, vmem],
        out_specs=vmem,
        scratch_shapes=[
            pltpu.VMEM((4, 3, width, third), jnp.bfloat16),
            pltpu.VMEM((2 * entries, width), jnp.bfloat16),
            pltpu.VMEM((3, third, width), jnp.float32),
            pltpu.VMEM((4, 3, 8, third), jnp.int32),
            pltpu.VMEM((4, 3, 8, third), jnp.float32),
            pltpu.VMEM((4, 3, 8, third), jnp.float32),
            pltpu.VMEM((nz, 3, 8, third), jnp.float32),
            dma((3,)), dma((3,)),
            *[dma((3 * PIECES,)) for _ in range(6)],
            dma((3,)), dma((3,)), dma((3,)), dma((3,)),
            dma((nz - 1,)), dma((nz - 1,)),
        ],
        compiler_params=pltpu.CompilerParams(
            collective_id=0, has_side_effects=True, vmem_limit_bytes=56 * 1024 * 1024
        ),
        cost_estimate=pl.CostEstimate(
            flops=2 * 4 * rows * 2 * entries * width,
            bytes_accessed=rows * width * 4 + entries * width * 2,
            transcendentals=4 * rows * 2 * entries,
        ),
    )(hidden_states, norm_gain.reshape(1, width), head_weight, goal)
    live = jnp.arange(rows, dtype=jnp.int32) < lengths[0]
    log_probs = jnp.where(live, scores[:, 0, :].reshape(rows), 0.0)
    entropies = jnp.where(live, scores[:, 1, :].reshape(rows), 0.0)
    return (log_probs, entropies)


def gathered(hidden_states, norm_gain, head_weight, target_ids, lengths):
    row_count = hidden_states.shape[0]
    scale = lax.rsqrt(jnp.mean(hidden_states * hidden_states, axis=1, keepdims=True) + epsilon)
    normed = (hidden_states * scale * norm_gain).astype(jnp.bfloat16)
    slice_width = head_weight.shape[0] * lax.axis_size("dp")
    goal_cols = target_ids - lax.axis_index("vocab") * slice_width
    live_mask = jnp.arange(row_count, dtype=jnp.int32) < lengths[0]
    logits = lax.dot_general(
        normed, lax.all_gather(head_weight, "dp", axis=0, tiled=True),
        (((1,), (1,)), ((), ())), preferred_element_type=jnp.float32,
    )
    columns = jnp.arange(logits.shape[1], dtype=jnp.int32)
    highest = jnp.max(logits, axis=1)
    weights = jnp.exp(logits - highest[:, None])
    matched = jnp.where(columns[None, :] == goal_cols[:, None], logits, 0.0)
    maxima = lax.pmax(highest, "vocab")
    factor = jnp.exp(highest - maxima)
    totals, tilted, target_logit = lax.psum(
        (
            jnp.sum(weights, axis=1) * factor,
            jnp.sum(weights * logits, axis=1) * factor,
            jnp.sum(matched, axis=1),
        ),
        "vocab",
    )
    log_total = maxima + jnp.log(totals)
    log_probs = jnp.where(live_mask, target_logit - log_total, 0.0)
    entropies = jnp.where(live_mask, log_total - tilted / totals, 0.0)
    return (log_probs, entropies)


def solution(mesh):
    ndp, nz = mesh.shape["dp"], mesh.shape["vocab"]

    def on_device(*args):
        rows, width = args[0].shape
        entries = args[2].shape[0]
        fits = (
            ndp == 8 and nz % 2 == 0 and rows % 768 == 0 and width % 128 == 0
            and 2 * entries % BLOCK == 0
            and 20 * rows * width + 4 * entries * width < 40 * 1024 * 1024
        )
        return fused(nz, *args) if fits else gathered(*args)

    in_specs = (P("dp", None), P(), P(("vocab", "dp"), None), P("dp"), P("dp"))
    out_specs = (P("dp"), P("dp"))
    return jax.shard_map(
        on_device, mesh=mesh, in_specs=in_specs, out_specs=out_specs, check_vma=False
    )
```

```python
import functools

import jax
import jax.numpy as jnp
from jax import lax
from jax.experimental import pallas as pl
from jax.experimental.pallas import tpu as pltpu
from jax.sharding import PartitionSpec as P

epsilon = 1e-05
lowest = -1e30
MESH = pl.DeviceIdType.MESH
BLOCK = 512
PIECES = 8
WINDOW = 5
FIRST = 3
STRIDE = 2


def merge(parts):
    top = parts[0][:, 0:1, :]
    for part in parts[1:]:
        top = jnp.maximum(top, part[:, 0:1, :])
    total = tilted = target = jnp.zeros_like(top)
    for part in parts:
        factor = jnp.exp(part[:, 0:1, :] - top)
        total = total + part[:, 1:2, :] * factor
        tilted = tilted + part[:, 2:3, :] * factor
        target = target + part[:, 3:4, :]
    return top, total, tilted, target


def rows_of(values, shape):
    axis = len(shape) - 2
    row = lax.broadcasted_iota(jnp.int32, shape, axis)
    tile = jnp.zeros(shape, jnp.float32)
    for i, value in enumerate(values):
        tile = jnp.where(row == i, value, tile)
    return tile


def kernel(nz, hid, gain, head, ids, lengths, log_probs, entropies, T, W, raw, goal, tgt, st, rs, rz,
           hid_sem, w_sem, xs, xr, ys, yr, zs, zr, gs, gr, ss, sr, vs, vr):
    dp = lax.axis_index("dp")
    z = lax.axis_index("vocab")
    core = lax.rem(dp, 2)
    xc = lax.rem(lax.div(dp, 2), 2)
    yc = lax.div(dp, 4)
    p = lax.rem(z, 2)
    q = p + 1
    s = 2 * p
    m = 2 - s
    near_core = (dp + 1 - 2 * core, z)
    near_x = (dp + 2 - 4 * xc, z)
    near_y = (dp + 4 - 8 * yc, z)
    near_d = (dp + 2 - 4 * xc + 4 - 8 * yc, z)
    near_z = (dp, z + 1 - 2 * p)
    far_z = [(dp, lax.rem(z + k, nz)) for k in range(1, nz)]
    partners = [near_core, near_x, near_y, near_d] + far_z

    width, third = T.shape[2:]
    size = width // PIECES
    waves = 3 * PIECES
    entries = head.shape[0]
    base = (z * lax.axis_size("dp") + dp - core) * entries

    for t in range(3):
        goal[t] = jnp.broadcast_to(ids[pl.ds(t * third, third)][None, :], (8, third))

    def load(t):
        return pltpu.make_async_copy(
            hid.at[pl.ds(t * third, third)], raw.at[t], hid_sem.at[t]
        )

    def send(src, dst, send_sem, recv_sem, where):
        return pltpu.make_async_remote_copy(
            src_ref=src, dst_ref=dst, send_sem=send_sem, recv_sem=recv_sem,
            device_id=where, device_id_type=MESH,
        )

    def piece(slot, t, k):
        return T.at[slot, t, pl.ds(lax.rem(k, PIECES) * size, size)]

    def X(k):
        g = lax.div(k, PIECES)
        d, t = lax.div(g, 2), q - lax.div(g + 1, 2)
        return send(piece(2 * d, t, k), piece(1 + 2 * d, t, k), xs.at[k], xr.at[k], near_x)

    def Y(k):
        g = lax.div(k, PIECES)
        d, t = lax.div(g, 2), p + lax.div(g + 1, 2)
        return send(piece(d, t, k), piece(2 + d, t, k), ys.at[k], yr.at[k], near_y)

    def Z(k):
        g = lax.div(k, PIECES)
        slot = jnp.where(g == 0, 2 - p, jnp.where(g == 1, 1 + p, 3))
        return send(piece(slot, s, k), piece(slot, s, k), zs.at[k], zr.at[k], near_z)

    def Z_in(k):
        g = lax.div(k, PIECES)
        slot = jnp.where(g == 0, 1 + p, jnp.where(g == 1, 2 - p, 3))
        return send(piece(slot, m, k), piece(slot, m, k), zs.at[k], zr.at[k], near_z)

    own_rows = pl.ds(core * entries, entries)
    other_rows = pl.ds((1 - core) * entries, entries)
    w_local = pltpu.make_async_copy(head, W.at[own_rows], w_sem.at[0])
    w_send = send(head, W.at[own_rows], w_sem.at[1], w_sem.at[2], near_core)
    w_in = send(head, W.at[other_rows], w_sem.at[1], w_sem.at[2], near_core)
    goals = [
        send(goal, tgt.at[j], gs.at[j - 1], gr.at[j - 1], where)
        for j, where in ((1, near_x), (2, near_y), (3, near_d))
    ]
    stats = [
        send(st.at[j], rs.at[j], ss.at[j - 1], sr.at[j - 1], where)
        for j, where in ((1, near_x), (2, near_y), (3, near_d))
    ]

    for t in (p, q, m):
        load(t).start()
    barrier = pltpu.get_barrier_semaphore()
    for where in partners:
        pl.semaphore_signal(barrier, inc=1, device_id=where, device_id_type=MESH)
    w_local.start()

    def normalise(t):
        load(t).wait()
        states = raw[t]
        scale = lax.rsqrt(jnp.mean(states * states, axis=1, keepdims=True) + epsilon)
        T[0, t] = (states * scale * gain[...][None, :]).astype(jnp.bfloat16).T

    normalise(p)
    pl.semaphore_wait(barrier, len(partners))
    for k in range(WINDOW):
        Y(k).start()
    w_send.start()
    normalise(q)
    for k in range(WINDOW):
        X(k).start()
    for copy in goals:
        copy.start()
    normalise(m)
    tgt[0] = goal[...]

    def unit(slot, t):
        wanted = tgt[slot, t, 0:1, :] - base
        zero = jnp.zeros((8, third), jnp.float32)
        top, total, tilted, target = jnp.full((8, third), lowest, jnp.float32), zero, zero, zero
        for i in range(W.shape[0] // BLOCK):
            logits = jnp.dot(
                W[pl.ds(i * BLOCK, BLOCK), :], T[slot, t], preferred_element_type=jnp.float32
            )
            entry = lax.broadcasted_iota(jnp.int32, logits.shape, 0)
            hit = jnp.where(entry == wanted - i * BLOCK, logits, 0.0)
            target = target + jnp.sum(hit.reshape(BLOCK // 8, 8, third), axis=0)
            logits = logits.reshape(BLOCK // 8, 8, third)
            higher = jnp.maximum(top, jnp.max(logits, axis=0))
            factor = jnp.exp(top - higher)
            weights = jnp.exp(logits - higher[None])
            total = total * factor + jnp.sum(weights, axis=0)
            tilted = tilted * factor + jnp.sum(weights * logits, axis=0)
            top = higher
        highest = jnp.max(top, axis=0, keepdims=True)
        factor = jnp.exp(top - highest)
        st[slot, t] = rows_of(
            (
                highest,
                jnp.sum(total * factor, axis=0, keepdims=True),
                jnp.sum(tilted * factor, axis=0, keepdims=True),
                jnp.sum(target, axis=0, keepdims=True),
            ),
            (8, third),
        )

    def pick(g, u):
        slot = jnp.where(g == 0, 0, jnp.where(g == 3, 3, 1 + u))
        t = jnp.where(g == 1, q - u, p + u)
        late = jnp.where(g == 1, 1 + p, jnp.where(g == 2, 2 - p, g))
        return jnp.where(u == 2, late, slot), jnp.where(u == 2, m, t)

    def step(k, carry):
        g, j = lax.div(k, PIECES), lax.rem(k, PIECES)
        tail = k >= waves
        u = jnp.where(tail, j, lax.div(j - FIRST, STRIDE))
        turn = tail | ((j >= FIRST) & (lax.rem(j - FIRST + PIECES * STRIDE, STRIDE) == 0))

        @pl.when(k < waves)
        def _():
            X(k).wait_recv()

        @pl.when(k + WINDOW < waves)
        def _():
            X(k + WINDOW).start()

        @pl.when(k < waves)
        def _():
            Y(k).wait_recv()

        @pl.when(k + WINDOW < waves)
        def _():
            Y(k + WINDOW).start()

        @pl.when(k < waves)
        def _():
            Z(k).start()

        @pl.when(k == FIRST)
        def _():
            w_local.wait()
            w_in.wait_recv()
            for copy in goals:
                copy.wait_recv()

        @pl.when(k == waves)
        def _():
            stats[0].start()
            stats[1].start()

        @pl.when(turn & (u == 2) & (g > 0))
        def _():
            def arrive(i, carry):
                Z_in((g - 1) * PIECES + i).wait_recv()
                return carry

            lax.fori_loop(0, PIECES, arrive, 0)

        @pl.when(turn)
        def _():
            unit(*pick(g, u))

        return carry

    lax.fori_loop(0, waves + 3, step, 0)
    stats[2].start()
    for copy in stats:
        copy.wait_recv()
    top, total, tilted, target = merge([st[0], rs[1], rs[2], rs[3]])
    rz[z] = rows_of((top, total, tilted, target), (3, 8, third))

    def V(k, source):
        return send(rz.at[source], rz.at[source], vs.at[k - 1], vr.at[k - 1], far_z[k - 1])

    for k in range(1, nz):
        V(k, z).start()
    for k in range(1, nz):
        V(k, lax.rem(z + nz - k, nz)).wait_recv()
    top, total, tilted, target = merge([rz[i] for i in range(nz)])
    log_total = top + jnp.log(total)
    chosen = target - log_total
    spread = log_total - tilted / total
    for t in range(3):
        slots = pl.ds(t * third, third)
        position = lax.broadcasted_iota(jnp.int32, (1, third), 1) + t * third
        live = position < lengths[0]
        log_probs[slots] = jnp.where(live, chosen[t], 0.0)[0]
        entropies[slots] = jnp.where(live, spread[t], 0.0)[0]

    w_send.wait_send()

    def sent(k, carry):
        X(k).wait_send()
        Y(k).wait_send()
        Z(k).wait_send()
        return carry

    lax.fori_loop(0, waves, sent, 0)
    for copy in goals + stats:
        copy.wait_send()
    for k in range(1, nz):
        V(k, z).wait_send()


def fused(nz, hidden_states, norm_gain, head_weight, target_ids, lengths):
    rows, width = hidden_states.shape
    entries = head_weight.shape[0]
    third = rows // 3
    dma = pltpu.SemaphoreType.DMA
    any_space = pl.BlockSpec(memory_space=pl.ANY)
    vmem = pl.BlockSpec(memory_space=pltpu.VMEM)
    return pl.pallas_call(
        functools.partial(kernel, nz),
        out_shape=(jax.ShapeDtypeStruct((rows,), jnp.float32),) * 2,
        in_specs=[any_space, vmem, any_space, vmem, pl.BlockSpec(memory_space=pltpu.SMEM)],
        out_specs=(vmem, vmem),
        scratch_shapes=[
            pltpu.VMEM((4, 3, width, third), jnp.bfloat16),
            pltpu.VMEM((2 * entries, width), jnp.bfloat16),
            pltpu.VMEM((3, third, width), jnp.float32),
            pltpu.VMEM((3, 8, third), jnp.int32),
            pltpu.VMEM((4, 3, 8, third), jnp.int32),
            pltpu.VMEM((4, 3, 8, third), jnp.float32),
            pltpu.VMEM((4, 3, 8, third), jnp.float32),
            pltpu.VMEM((nz, 3, 8, third), jnp.float32),
            dma((3,)), dma((3,)),
            *[dma((3 * PIECES,)) for _ in range(6)],
            dma((3,)), dma((3,)), dma((3,)), dma((3,)),
            dma((nz - 1,)), dma((nz - 1,)),
        ],
        compiler_params=pltpu.CompilerParams(
            collective_id=0, has_side_effects=True, vmem_limit_bytes=56 * 1024 * 1024
        ),
        cost_estimate=pl.CostEstimate(
            flops=2 * 4 * rows * 2 * entries * width,
            bytes_accessed=rows * width * 4 + entries * width * 2,
            transcendentals=4 * rows * 2 * entries,
        ),
    )(hidden_states, norm_gain, head_weight, target_ids, lengths)


def gathered(hidden_states, norm_gain, head_weight, target_ids, lengths):
    row_count = hidden_states.shape[0]
    scale = lax.rsqrt(jnp.mean(hidden_states * hidden_states, axis=1, keepdims=True) + epsilon)
    normed = (hidden_states * scale * norm_gain).astype(jnp.bfloat16)
    slice_width = head_weight.shape[0] * lax.axis_size("dp")
    goal_cols = target_ids - lax.axis_index("vocab") * slice_width
    live_mask = jnp.arange(row_count, dtype=jnp.int32) < lengths[0]
    logits = lax.dot_general(
        normed, lax.all_gather(head_weight, "dp", axis=0, tiled=True),
        (((1,), (1,)), ((), ())), preferred_element_type=jnp.float32,
    )
    columns = jnp.arange(logits.shape[1], dtype=jnp.int32)
    highest = jnp.max(logits, axis=1)
    weights = jnp.exp(logits - highest[:, None])
    matched = jnp.where(columns[None, :] == goal_cols[:, None], logits, 0.0)
    maxima = lax.pmax(highest, "vocab")
    factor = jnp.exp(highest - maxima)
    totals, tilted, target_logit = lax.psum(
        (
            jnp.sum(weights, axis=1) * factor,
            jnp.sum(weights * logits, axis=1) * factor,
            jnp.sum(matched, axis=1),
        ),
        "vocab",
    )
    log_total = maxima + jnp.log(totals)
    log_probs = jnp.where(live_mask, target_logit - log_total, 0.0)
    entropies = jnp.where(live_mask, log_total - tilted / totals, 0.0)
    return (log_probs, entropies)


def solution(mesh):
    ndp, nz = mesh.shape["dp"], mesh.shape["vocab"]

    def on_device(*args):
        rows, width = args[0].shape
        entries = args[2].shape[0]
        fits = (
            ndp == 8 and nz % 2 == 0 and rows % 768 == 0 and width % 128 == 0
            and 2 * entries % BLOCK == 0
            and 20 * rows * width + 4 * entries * width < 40 * 1024 * 1024
        )
        return fused(nz, *args) if fits else gathered(*args)

    in_specs = (P("dp", None), P(), P(("vocab", "dp"), None), P("dp"), P("dp"))
    out_specs = (P("dp"), P("dp"))
    return jax.shard_map(
        on_device, mesh=mesh, in_specs=in_specs, out_specs=out_specs, check_vma=False
    )
```

```python
import functools

import jax
import jax.numpy as jnp
from jax import lax
from jax.experimental import pallas as pl
from jax.experimental.pallas import tpu as pltpu
from jax.sharding import PartitionSpec as P

epsilon = 1e-05
lowest = -1e30
MESH = pl.DeviceIdType.MESH
BLOCK = 1024
PIECES = 8
WINDOW = 3
FIRST = 1
STRIDE = 2


def merge(parts):
    top = parts[0][:, 0:1, :]
    for part in parts[1:]:
        top = jnp.maximum(top, part[:, 0:1, :])
    total = tilted = target = jnp.zeros_like(top)
    for part in parts:
        factor = jnp.exp(part[:, 0:1, :] - top)
        total = total + part[:, 1:2, :] * factor
        tilted = tilted + part[:, 2:3, :] * factor
        target = target + part[:, 3:4, :]
    return top, total, tilted, target


def rows_of(values, shape):
    axis = len(shape) - 2
    row = lax.broadcasted_iota(jnp.int32, shape, axis)
    tile = jnp.zeros(shape, jnp.float32)
    for i, value in enumerate(values):
        tile = jnp.where(row == i, value, tile)
    return tile


def kernel(nz, hid, gain, head, ids, lengths, log_probs, entropies, T, W, raw, goal, tgt, st, rs, rz,
           hid_sem, w_sem, xs, xr, ys, yr, zs, zr, gs, gr, ss, sr, vs, vr):
    dp = lax.axis_index("dp")
    z = lax.axis_index("vocab")
    core = lax.rem(dp, 2)
    xc = lax.rem(lax.div(dp, 2), 2)
    yc = lax.div(dp, 4)
    p = lax.rem(z, 2)
    q = p + 1
    s = 2 * p
    m = 2 - s
    near_core = (dp + 1 - 2 * core, z)
    near_x = (dp + 2 - 4 * xc, z)
    near_y = (dp + 4 - 8 * yc, z)
    near_d = (dp + 2 - 4 * xc + 4 - 8 * yc, z)
    near_z = (dp, z + 1 - 2 * p)
    far_z = [(dp, lax.rem(z + k, nz)) for k in range(1, nz)]
    partners = [near_core, near_x, near_y, near_d] + far_z

    width, third = T.shape[2:]
    size = width // PIECES
    waves = 3 * PIECES
    entries = head.shape[0]
    base = (z * lax.axis_size("dp") + dp - core) * entries

    for t in range(3):
        goal[t] = jnp.broadcast_to(ids[pl.ds(t * third, third)][None, :], (8, third))

    def load(t):
        return pltpu.make_async_copy(
            hid.at[pl.ds(t * third, third)], raw.at[t], hid_sem.at[t]
        )

    def send(src, dst, send_sem, recv_sem, where):
        return pltpu.make_async_remote_copy(
            src_ref=src, dst_ref=dst, send_sem=send_sem, recv_sem=recv_sem,
            device_id=where, device_id_type=MESH,
        )

    def piece(slot, t, k):
        return T.at[slot, t, pl.ds(lax.rem(k, PIECES) * size, size)]

    def X(k):
        g = lax.div(k, PIECES)
        d, t = lax.div(g, 2), q - lax.div(g + 1, 2)
        return send(piece(2 * d, t, k), piece(1 + 2 * d, t, k), xs.at[k], xr.at[k], near_x)

    def Y(k):
        g = lax.div(k, PIECES)
        d, t = lax.div(g, 2), p + lax.div(g + 1, 2)
        return send(piece(d, t, k), piece(2 + d, t, k), ys.at[k], yr.at[k], near_y)

    def Z(k):
        g = lax.div(k, PIECES)
        slot = jnp.where(g == 0, 2 - p, jnp.where(g == 1, 1 + p, 3))
        return send(piece(slot, s, k), piece(slot, s, k), zs.at[k], zr.at[k], near_z)

    def Z_in(k):
        g = lax.div(k, PIECES)
        slot = jnp.where(g == 0, 1 + p, jnp.where(g == 1, 2 - p, 3))
        return send(piece(slot, m, k), piece(slot, m, k), zs.at[k], zr.at[k], near_z)

    own_rows = pl.ds(core * entries, entries)
    other_rows = pl.ds((1 - core) * entries, entries)
    w_local = pltpu.make_async_copy(head, W.at[own_rows], w_sem.at[0])
    w_send = send(head, W.at[own_rows], w_sem.at[1], w_sem.at[2], near_core)
    w_in = send(head, W.at[other_rows], w_sem.at[1], w_sem.at[2], near_core)
    goals = [
        send(goal, tgt.at[j], gs.at[j - 1], gr.at[j - 1], where)
        for j, where in ((1, near_x), (2, near_y), (3, near_d))
    ]
    stats = [
        send(st.at[j], rs.at[j], ss.at[j - 1], sr.at[j - 1], where)
        for j, where in ((1, near_x), (2, near_y), (3, near_d))
    ]

    for t in (p, q, m):
        load(t).start()
    barrier = pltpu.get_barrier_semaphore()
    for where in partners:
        pl.semaphore_signal(barrier, inc=1, device_id=where, device_id_type=MESH)
    w_local.start()

    def normalise(t):
        load(t).wait()
        states = raw[t]
        scale = lax.rsqrt(jnp.mean(states * states, axis=1, keepdims=True) + epsilon)
        T[0, t] = (states * scale * gain[...][None, :]).astype(jnp.bfloat16).T

    normalise(p)
    pl.semaphore_wait(barrier, len(partners))
    for k in range(WINDOW):
        Y(k).start()
    w_send.start()
    normalise(q)
    for k in range(WINDOW):
        X(k).start()
    for copy in goals:
        copy.start()
    normalise(m)
    tgt[0] = goal[...]

    def unit(slot, t):
        wanted = tgt[slot, t, 0:1, :] - base
        zero = jnp.zeros((8, third), jnp.float32)
        top, total, tilted, target = jnp.full((8, third), lowest, jnp.float32), zero, zero, zero
        for i in range(W.shape[0] // BLOCK):
            logits = jnp.dot(
                W[pl.ds(i * BLOCK, BLOCK), :], T[slot, t], preferred_element_type=jnp.float32
            )
            entry = lax.broadcasted_iota(jnp.int32, logits.shape, 0)
            hit = jnp.where(entry == wanted - i * BLOCK, logits, 0.0)
            target = target + jnp.sum(hit.reshape(BLOCK // 8, 8, third), axis=0)
            logits = logits.reshape(BLOCK // 8, 8, third)
            higher = jnp.maximum(top, jnp.max(logits, axis=0))
            factor = jnp.exp(top - higher)
            weights = jnp.exp(logits - higher[None])
            total = total * factor + jnp.sum(weights, axis=0)
            tilted = tilted * factor + jnp.sum(weights * logits, axis=0)
            top = higher
        highest = jnp.max(top, axis=0, keepdims=True)
        factor = jnp.exp(top - highest)
        st[slot, t] = rows_of(
            (
                highest,
                jnp.sum(total * factor, axis=0, keepdims=True),
                jnp.sum(tilted * factor, axis=0, keepdims=True),
                jnp.sum(target, axis=0, keepdims=True),
            ),
            (8, third),
        )

    def pick(g, u):
        slot = jnp.where(g == 0, 0, jnp.where(g == 3, 3, 1 + u))
        t = jnp.where(g == 1, q - u, p + u)
        late = jnp.where(g == 1, 1 + p, jnp.where(g == 2, 2 - p, g))
        return jnp.where(u == 2, late, slot), jnp.where(u == 2, m, t)

    def step(k, carry):
        g, j = lax.div(k, PIECES), lax.rem(k, PIECES)
        tail = k >= waves
        u = jnp.where(tail, j, lax.div(j - FIRST, STRIDE))
        turn = tail | ((j >= FIRST) & (u < 3) & (lax.rem(j - FIRST + PIECES * STRIDE, STRIDE) == 0))

        @pl.when(k < waves)
        def _():
            X(k).wait_recv()

        @pl.when(k + WINDOW < waves)
        def _():
            X(k + WINDOW).start()

        @pl.when(k < waves)
        def _():
            Y(k).wait_recv()

        @pl.when(k + WINDOW < waves)
        def _():
            Y(k + WINDOW).start()

        @pl.when(k < waves)
        def _():
            Z(k).start()

        @pl.when(k == FIRST)
        def _():
            w_local.wait()
            w_in.wait_recv()
            for copy in goals:
                copy.wait_recv()

        @pl.when(k == waves)
        def _():
            stats[0].start()
            stats[1].start()

        @pl.when(turn & (u == 2) & (g > 0))
        def _():
            def arrive(i, carry):
                Z_in((g - 1) * PIECES + i).wait_recv()
                return carry

            lax.fori_loop(0, PIECES, arrive, 0)

        @pl.when(turn)
        def _():
            unit(*pick(g, u))

        return carry

    lax.fori_loop(0, waves + 3, step, 0)
    stats[2].start()
    for copy in stats:
        copy.wait_recv()
    top, total, tilted, target = merge([st[0], rs[1], rs[2], rs[3]])
    rz[z] = rows_of((top, total, tilted, target), (3, 8, third))

    def V(k, source):
        return send(rz.at[source], rz.at[source], vs.at[k - 1], vr.at[k - 1], far_z[k - 1])

    for k in range(1, nz):
        V(k, z).start()
    for k in range(1, nz):
        V(k, lax.rem(z + nz - k, nz)).wait_recv()
    top, total, tilted, target = merge([rz[i] for i in range(nz)])
    log_total = top + jnp.log(total)
    chosen = target - log_total
    spread = log_total - tilted / total
    for t in range(3):
        slots = pl.ds(t * third, third)
        position = lax.broadcasted_iota(jnp.int32, (1, third), 1) + t * third
        live = position < lengths[0]
        log_probs[slots] = jnp.where(live, chosen[t], 0.0)[0]
        entropies[slots] = jnp.where(live, spread[t], 0.0)[0]

    w_send.wait_send()

    def sent(k, carry):
        X(k).wait_send()
        Y(k).wait_send()
        Z(k).wait_send()
        return carry

    lax.fori_loop(0, waves, sent, 0)
    for copy in goals + stats:
        copy.wait_send()
    for k in range(1, nz):
        V(k, z).wait_send()


def fused(nz, hidden_states, norm_gain, head_weight, target_ids, lengths):
    rows, width = hidden_states.shape
    entries = head_weight.shape[0]
    third = rows // 3
    dma = pltpu.SemaphoreType.DMA
    any_space = pl.BlockSpec(memory_space=pl.ANY)
    vmem = pl.BlockSpec(memory_space=pltpu.VMEM)
    return pl.pallas_call(
        functools.partial(kernel, nz),
        out_shape=(jax.ShapeDtypeStruct((rows,), jnp.float32),) * 2,
        in_specs=[any_space, vmem, any_space, vmem, pl.BlockSpec(memory_space=pltpu.SMEM)],
        out_specs=(vmem, vmem),
        scratch_shapes=[
            pltpu.VMEM((4, 3, width, third), jnp.bfloat16),
            pltpu.VMEM((2 * entries, width), jnp.bfloat16),
            pltpu.VMEM((3, third, width), jnp.float32),
            pltpu.VMEM((3, 8, third), jnp.int32),
            pltpu.VMEM((4, 3, 8, third), jnp.int32),
            pltpu.VMEM((4, 3, 8, third), jnp.float32),
            pltpu.VMEM((4, 3, 8, third), jnp.float32),
            pltpu.VMEM((nz, 3, 8, third), jnp.float32),
            dma((3,)), dma((3,)),
            *[dma((3 * PIECES,)) for _ in range(6)],
            dma((3,)), dma((3,)), dma((3,)), dma((3,)),
            dma((nz - 1,)), dma((nz - 1,)),
        ],
        compiler_params=pltpu.CompilerParams(
            collective_id=0, has_side_effects=True, vmem_limit_bytes=56 * 1024 * 1024
        ),
        cost_estimate=pl.CostEstimate(
            flops=2 * 4 * rows * 2 * entries * width,
            bytes_accessed=rows * width * 4 + entries * width * 2,
            transcendentals=4 * rows * 2 * entries,
        ),
    )(hidden_states, norm_gain, head_weight, target_ids, lengths)


def gathered(hidden_states, norm_gain, head_weight, target_ids, lengths):
    row_count = hidden_states.shape[0]
    scale = lax.rsqrt(jnp.mean(hidden_states * hidden_states, axis=1, keepdims=True) + epsilon)
    normed = (hidden_states * scale * norm_gain).astype(jnp.bfloat16)
    slice_width = head_weight.shape[0] * lax.axis_size("dp")
    goal_cols = target_ids - lax.axis_index("vocab") * slice_width
    live_mask = jnp.arange(row_count, dtype=jnp.int32) < lengths[0]
    logits = lax.dot_general(
        normed, lax.all_gather(head_weight, "dp", axis=0, tiled=True),
        (((1,), (1,)), ((), ())), preferred_element_type=jnp.float32,
    )
    columns = jnp.arange(logits.shape[1], dtype=jnp.int32)
    highest = jnp.max(logits, axis=1)
    weights = jnp.exp(logits - highest[:, None])
    matched = jnp.where(columns[None, :] == goal_cols[:, None], logits, 0.0)
    maxima = lax.pmax(highest, "vocab")
    factor = jnp.exp(highest - maxima)
    totals, tilted, target_logit = lax.psum(
        (
            jnp.sum(weights, axis=1) * factor,
            jnp.sum(weights * logits, axis=1) * factor,
            jnp.sum(matched, axis=1),
        ),
        "vocab",
    )
    log_total = maxima + jnp.log(totals)
    log_probs = jnp.where(live_mask, target_logit - log_total, 0.0)
    entropies = jnp.where(live_mask, log_total - tilted / totals, 0.0)
    return (log_probs, entropies)


def solution(mesh):
    ndp, nz = mesh.shape["dp"], mesh.shape["vocab"]

    def on_device(*args):
        rows, width = args[0].shape
        entries = args[2].shape[0]
        fits = (
            ndp == 8 and nz % 2 == 0 and rows % 768 == 0 and width % 128 == 0
            and 2 * entries % BLOCK == 0
            and 20 * rows * width + 4 * entries * width < 40 * 1024 * 1024
        )
        return fused(nz, *args) if fits else gathered(*args)

    in_specs = (P("dp", None), P(), P(("vocab", "dp"), None), P("dp"), P("dp"))
    out_specs = (P("dp"), P("dp"))
    return jax.shard_map(
        on_device, mesh=mesh, in_specs=in_specs, out_specs=out_specs, check_vma=False
    )
```

```python
import functools

import jax
import jax.numpy as jnp
from jax import lax
from jax.experimental import pallas as pl
from jax.experimental.pallas import tpu as pltpu
from jax.sharding import PartitionSpec as P

epsilon = 1e-05
lowest = -1e30
MESH = pl.DeviceIdType.MESH
BLOCK = 256
PIECES = 4
WINDOW = 2
FIRST = 0
STRIDE = 1


def merge(parts):
    top = parts[0][:, 0:1, :]
    for part in parts[1:]:
        top = jnp.maximum(top, part[:, 0:1, :])
    total = tilted = target = jnp.zeros_like(top)
    for part in parts:
        factor = jnp.exp(part[:, 0:1, :] - top)
        total = total + part[:, 1:2, :] * factor
        tilted = tilted + part[:, 2:3, :] * factor
        target = target + part[:, 3:4, :]
    return top, total, tilted, target


def rows_of(values, shape):
    axis = len(shape) - 2
    row = lax.broadcasted_iota(jnp.int32, shape, axis)
    tile = jnp.zeros(shape, jnp.float32)
    for i, value in enumerate(values):
        tile = jnp.where(row == i, value, tile)
    return tile


def kernel(nz, hid, gain, head, ids, lengths, log_probs, entropies, T, W, raw, goal, tgt, st, rs, rz,
           hid_sem, w_sem, xs, xr, ys, yr, zs, zr, gs, gr, ss, sr, vs, vr):
    dp = lax.axis_index("dp")
    z = lax.axis_index("vocab")
    core = lax.rem(dp, 2)
    xc = lax.rem(lax.div(dp, 2), 2)
    yc = lax.div(dp, 4)
    p = lax.rem(z, 2)
    q = p + 1
    s = 2 * p
    m = 2 - s
    near_core = (dp + 1 - 2 * core, z)
    near_x = (dp + 2 - 4 * xc, z)
    near_y = (dp + 4 - 8 * yc, z)
    near_d = (dp + 2 - 4 * xc + 4 - 8 * yc, z)
    near_z = (dp, z + 1 - 2 * p)
    far_z = [(dp, lax.rem(z + k, nz)) for k in range(1, nz)]
    partners = [near_core, near_x, near_y, near_d] + far_z

    width, third = T.shape[2:]
    size = width // PIECES
    waves = 3 * PIECES
    entries = head.shape[0]
    base = (z * lax.axis_size("dp") + dp - core) * entries

    for t in range(3):
        goal[t] = jnp.broadcast_to(ids[pl.ds(t * third, third)][None, :], (8, third))

    def load(t):
        return pltpu.make_async_copy(
            hid.at[pl.ds(t * third, third)], raw.at[t], hid_sem.at[t]
        )

    def send(src, dst, send_sem, recv_sem, where):
        return pltpu.make_async_remote_copy(
            src_ref=src, dst_ref=dst, send_sem=send_sem, recv_sem=recv_sem,
            device_id=where, device_id_type=MESH,
        )

    def piece(slot, t, k):
        return T.at[slot, t, pl.ds(lax.rem(k, PIECES) * size, size)]

    def X(k):
        g = lax.div(k, PIECES)
        d, t = lax.div(g, 2), q - lax.div(g + 1, 2)
        return send(piece(2 * d, t, k), piece(1 + 2 * d, t, k), xs.at[k], xr.at[k], near_x)

    def Y(k):
        g = lax.div(k, PIECES)
        d, t = lax.div(g, 2), p + lax.div(g + 1, 2)
        return send(piece(d, t, k), piece(2 + d, t, k), ys.at[k], yr.at[k], near_y)

    def Z(k):
        g = lax.div(k, PIECES)
        slot = jnp.where(g == 0, 2 - p, jnp.where(g == 1, 1 + p, 3))
        return send(piece(slot, s, k), piece(slot, s, k), zs.at[k], zr.at[k], near_z)

    def Z_in(k):
        g = lax.div(k, PIECES)
        slot = jnp.where(g == 0, 1 + p, jnp.where(g == 1, 2 - p, 3))
        return send(piece(slot, m, k), piece(slot, m, k), zs.at[k], zr.at[k], near_z)

    own_rows = pl.ds(core * entries, entries)
    other_rows = pl.ds((1 - core) * entries, entries)
    w_local = pltpu.make_async_copy(head, W.at[own_rows], w_sem.at[0])
    w_send = send(head, W.at[own_rows], w_sem.at[1], w_sem.at[2], near_core)
    w_in = send(head, W.at[other_rows], w_sem.at[1], w_sem.at[2], near_core)
    goals = [
        send(goal, tgt.at[j], gs.at[j - 1], gr.at[j - 1], where)
        for j, where in ((1, near_x), (2, near_y), (3, near_d))
    ]
    stats = [
        send(st.at[j], rs.at[j], ss.at[j - 1], sr.at[j - 1], where)
        for j, where in ((1, near_x), (2, near_y), (3, near_d))
    ]

    for t in (p, q, m):
        load(t).start()
    barrier = pltpu.get_barrier_semaphore()
    for where in partners:
        pl.semaphore_signal(barrier, inc=1, device_id=where, device_id_type=MESH)
    w_local.start()

    def normalise(t):
        load(t).wait()
        states = raw[t]
        scale = lax.rsqrt(jnp.mean(states * states, axis=1, keepdims=True) + epsilon)
        T[0, t] = (states * scale * gain[...][None, :]).astype(jnp.bfloat16).T

    normalise(p)
    pl.semaphore_wait(barrier, len(partners))
    Y(0).start()
    w_send.start()
    normalise(q)
    X(0).start()
    for copy in goals:
        copy.start()
    normalise(m)
    tgt[0] = goal[...]
    for k in range(1, WINDOW):
        Y(k).start()
        X(k).start()

    def unit(slot, t):
        wanted = tgt[slot, t, 0:1, :] - base
        zero = jnp.zeros((8, third), jnp.float32)
        top, total, tilted, target = jnp.full((8, third), lowest, jnp.float32), zero, zero, zero
        def score(i):
            return jnp.dot(
                W[pl.ds(i * BLOCK, BLOCK), :], T[slot, t], preferred_element_type=jnp.float32
            )

        blocks = W.shape[0] // BLOCK
        following = score(0)
        for i in range(blocks):
            logits = following
            if i + 1 < blocks:
                following = score(i + 1)
            entry = lax.broadcasted_iota(jnp.int32, logits.shape, 0)
            hit = jnp.where(entry == wanted - i * BLOCK, logits, 0.0)
            target = target + jnp.sum(hit.reshape(BLOCK // 8, 8, third), axis=0)
            logits = logits.reshape(BLOCK // 8, 8, third)
            higher = jnp.maximum(top, jnp.max(logits, axis=0))
            factor = jnp.exp(top - higher)
            weights = jnp.exp(logits - higher[None])
            total = total * factor + jnp.sum(weights, axis=0)
            tilted = tilted * factor + jnp.sum(weights * logits, axis=0)
            top = higher
        highest = jnp.max(top, axis=0, keepdims=True)
        factor = jnp.exp(top - highest)
        st[slot, t] = rows_of(
            (
                highest,
                jnp.sum(total * factor, axis=0, keepdims=True),
                jnp.sum(tilted * factor, axis=0, keepdims=True),
                jnp.sum(target, axis=0, keepdims=True),
            ),
            (8, third),
        )

    def pick(g, u):
        slot = jnp.where(g == 0, 0, jnp.where(g == 3, 3, 1 + u))
        t = jnp.where(g == 1, q - u, p + u)
        late = jnp.where(g == 1, 1 + p, jnp.where(g == 2, 2 - p, g))
        return jnp.where(u == 2, late, slot), jnp.where(u == 2, m, t)

    def step(k, carry):
        g, j = lax.div(k, PIECES), lax.rem(k, PIECES)
        tail = k >= waves
        u = jnp.where(tail, j, lax.div(j - FIRST, STRIDE))
        turn = tail | ((j >= FIRST) & (u < 3) & (lax.rem(j - FIRST + PIECES * STRIDE, STRIDE) == 0))

        @pl.when(k < waves)
        def _():
            X(k).wait_recv()

        @pl.when(k + WINDOW < waves)
        def _():
            X(k + WINDOW).start()

        @pl.when(k < waves)
        def _():
            Y(k).wait_recv()

        @pl.when(k + WINDOW < waves)
        def _():
            Y(k + WINDOW).start()

        @pl.when(k < waves)
        def _():
            Z(k).start()

        @pl.when(k == FIRST)
        def _():
            w_local.wait()
            w_in.wait_recv()
            for copy in goals:
                copy.wait_recv()

        @pl.when(k == waves)
        def _():
            stats[0].start()
            stats[1].start()

        @pl.when(turn & (u == 2) & (g > 0))
        def _():
            def arrive(i, carry):
                Z_in((g - 1) * PIECES + i).wait_recv()
                return carry

            lax.fori_loop(0, PIECES, arrive, 0)

        @pl.when(turn)
        def _():
            unit(*pick(g, u))

        return carry

    lax.fori_loop(0, waves + 3, step, 0)
    stats[2].start()
    for copy in stats:
        copy.wait_recv()
    top, total, tilted, target = merge([st[0], rs[1], rs[2], rs[3]])
    rz[z] = rows_of((top, total, tilted, target), (3, 8, third))

    def V(k, source):
        return send(rz.at[source], rz.at[source], vs.at[k - 1], vr.at[k - 1], far_z[k - 1])

    for k in range(1, nz):
        V(k, z).start()
    for k in range(1, nz):
        V(k, lax.rem(z + nz - k, nz)).wait_recv()
    top, total, tilted, target = merge([rz[i] for i in range(nz)])
    log_total = top + jnp.log(total)
    chosen = target - log_total
    spread = log_total - tilted / total
    for t in range(3):
        slots = pl.ds(t * third, third)
        position = lax.broadcasted_iota(jnp.int32, (1, third), 1) + t * third
        live = position < lengths[0]
        log_probs[slots] = jnp.where(live, chosen[t], 0.0)[0]
        entropies[slots] = jnp.where(live, spread[t], 0.0)[0]

    w_send.wait_send()

    def sent(k, carry):
        X(k).wait_send()
        Y(k).wait_send()
        Z(k).wait_send()
        return carry

    lax.fori_loop(0, waves, sent, 0)
    for copy in goals + stats:
        copy.wait_send()
    for k in range(1, nz):
        V(k, z).wait_send()


def fused(nz, hidden_states, norm_gain, head_weight, target_ids, lengths):
    rows, width = hidden_states.shape
    entries = head_weight.shape[0]
    third = rows // 3
    dma = pltpu.SemaphoreType.DMA
    any_space = pl.BlockSpec(memory_space=pl.ANY)
    vmem = pl.BlockSpec(memory_space=pltpu.VMEM)
    return pl.pallas_call(
        functools.partial(kernel, nz),
        out_shape=(jax.ShapeDtypeStruct((rows,), jnp.float32),) * 2,
        in_specs=[any_space, vmem, any_space, vmem, pl.BlockSpec(memory_space=pltpu.SMEM)],
        out_specs=(vmem, vmem),
        scratch_shapes=[
            pltpu.VMEM((4, 3, width, third), jnp.bfloat16),
            pltpu.VMEM((2 * entries, width), jnp.bfloat16),
            pltpu.VMEM((3, third, width), jnp.float32),
            pltpu.VMEM((3, 8, third), jnp.int32),
            pltpu.VMEM((4, 3, 8, third), jnp.int32),
            pltpu.VMEM((4, 3, 8, third), jnp.float32),
            pltpu.VMEM((4, 3, 8, third), jnp.float32),
            pltpu.VMEM((nz, 3, 8, third), jnp.float32),
            dma((3,)), dma((3,)),
            *[dma((3 * PIECES,)) for _ in range(6)],
            dma((3,)), dma((3,)), dma((3,)), dma((3,)),
            dma((nz - 1,)), dma((nz - 1,)),
        ],
        compiler_params=pltpu.CompilerParams(
            collective_id=0, has_side_effects=True, vmem_limit_bytes=56 * 1024 * 1024
        ),
        cost_estimate=pl.CostEstimate(
            flops=2 * 4 * rows * 2 * entries * width,
            bytes_accessed=rows * width * 4 + entries * width * 2,
            transcendentals=4 * rows * 2 * entries,
        ),
    )(hidden_states, norm_gain, head_weight, target_ids, lengths)


def gathered(hidden_states, norm_gain, head_weight, target_ids, lengths):
    row_count = hidden_states.shape[0]
    scale = lax.rsqrt(jnp.mean(hidden_states * hidden_states, axis=1, keepdims=True) + epsilon)
    normed = (hidden_states * scale * norm_gain).astype(jnp.bfloat16)
    slice_width = head_weight.shape[0] * lax.axis_size("dp")
    goal_cols = target_ids - lax.axis_index("vocab") * slice_width
    live_mask = jnp.arange(row_count, dtype=jnp.int32) < lengths[0]
    logits = lax.dot_general(
        normed, lax.all_gather(head_weight, "dp", axis=0, tiled=True),
        (((1,), (1,)), ((), ())), preferred_element_type=jnp.float32,
    )
    columns = jnp.arange(logits.shape[1], dtype=jnp.int32)
    highest = jnp.max(logits, axis=1)
    weights = jnp.exp(logits - highest[:, None])
    matched = jnp.where(columns[None, :] == goal_cols[:, None], logits, 0.0)
    maxima = lax.pmax(highest, "vocab")
    factor = jnp.exp(highest - maxima)
    totals, tilted, target_logit = lax.psum(
        (
            jnp.sum(weights, axis=1) * factor,
            jnp.sum(weights * logits, axis=1) * factor,
            jnp.sum(matched, axis=1),
        ),
        "vocab",
    )
    log_total = maxima + jnp.log(totals)
    log_probs = jnp.where(live_mask, target_logit - log_total, 0.0)
    entropies = jnp.where(live_mask, log_total - tilted / totals, 0.0)
    return (log_probs, entropies)


def solution(mesh):
    ndp, nz = mesh.shape["dp"], mesh.shape["vocab"]

    def on_device(*args):
        rows, width = args[0].shape
        entries = args[2].shape[0]
        fits = (
            ndp == 8 and nz % 2 == 0 and rows % 768 == 0 and width % 128 == 0
            and 2 * entries % BLOCK == 0
            and 20 * rows * width + 4 * entries * width < 40 * 1024 * 1024
        )
        return fused(nz, *args) if fits else gathered(*args)

    in_specs = (P("dp", None), P(), P(("vocab", "dp"), None), P("dp"), P("dp"))
    out_specs = (P("dp"), P("dp"))
    return jax.shard_map(
        on_device, mesh=mesh, in_specs=in_specs, out_specs=out_specs, check_vma=False
    )
```

```python
import functools

import jax
import jax.numpy as jnp
from jax import lax
from jax.experimental import pallas as pl
from jax.experimental.pallas import tpu as pltpu
from jax.sharding import PartitionSpec as P

epsilon = 1e-05
lowest = -1e30
MESH = pl.DeviceIdType.MESH
BLOCK = 256
PIECES = 4
WINDOW = 2


def merge(parts):
    top = parts[0][:, 0:1, :]
    for part in parts[1:]:
        top = jnp.maximum(top, part[:, 0:1, :])
    total = tilted = target = jnp.zeros_like(top)
    for part in parts:
        factor = jnp.exp(part[:, 0:1, :] - top)
        total = total + part[:, 1:2, :] * factor
        tilted = tilted + part[:, 2:3, :] * factor
        target = target + part[:, 3:4, :]
    return top, total, tilted, target


def rows_of(values, shape):
    axis = len(shape) - 2
    row = lax.broadcasted_iota(jnp.int32, shape, axis)
    tile = jnp.zeros(shape, jnp.float32)
    for i, value in enumerate(values):
        tile = jnp.where(row == i, value, tile)
    return tile


def kernel(nz, hid, gain, head, ids, lengths, log_probs, entropies, T, W, raw, begun, goal, tgt, st, rs, rz,
           hid_sem, w_sem, xs, xr, ys, yr, zs, zr, gs, gr, ss, sr, vs, vr):
    dp = lax.axis_index("dp")
    z = lax.axis_index("vocab")
    core = lax.rem(dp, 2)
    xc = lax.rem(lax.div(dp, 2), 2)
    yc = lax.div(dp, 4)
    p = lax.rem(z, 2)
    q = p + 1
    s = 2 * p
    m = 2 - s
    near_core = (dp + 1 - 2 * core, z)
    near_x = (dp + 2 - 4 * xc, z)
    near_y = (dp + 4 - 8 * yc, z)
    near_d = (dp + 2 - 4 * xc + 4 - 8 * yc, z)
    near_z = (dp, z + 1 - 2 * p)
    far_z = [(dp, lax.rem(z + k, nz)) for k in range(1, nz)]
    partners = [near_core, near_x, near_y, near_d] + far_z

    width, third = T.shape[2:]
    size = width // PIECES
    waves = 3 * PIECES
    entries = head.shape[0]
    base = (z * lax.axis_size("dp") + dp - core) * entries

    for t in range(3):
        goal[t] = jnp.broadcast_to(ids[pl.ds(t * third, third)][None, :], (8, third))

    def load(t):
        return pltpu.make_async_copy(
            hid.at[pl.ds(t * third, third)], raw.at[t], hid_sem.at[t]
        )

    def send(src, dst, send_sem, recv_sem, where):
        return pltpu.make_async_remote_copy(
            src_ref=src, dst_ref=dst, send_sem=send_sem, recv_sem=recv_sem,
            device_id=where, device_id_type=MESH,
        )

    def piece(slot, t, k):
        return T.at[slot, t, pl.ds(lax.rem(k, PIECES) * size, size)]

    def X(k):
        g = lax.div(k, PIECES)
        d, t = lax.div(g, 2), q - lax.div(g + 1, 2)
        return send(piece(2 * d, t, k), piece(1 + 2 * d, t, k), xs.at[k], xr.at[k], near_x)

    def Y(k):
        g = lax.div(k, PIECES)
        d, t = lax.div(g, 2), p + lax.div(g + 1, 2)
        return send(piece(d, t, k), piece(2 + d, t, k), ys.at[k], yr.at[k], near_y)

    def Z(k):
        g = lax.div(k, PIECES)
        slot = jnp.where(g == 0, 2 - p, jnp.where(g == 1, 1 + p, 3))
        return send(piece(slot, s, k), piece(slot, s, k), zs.at[k], zr.at[k], near_z)

    def Z_in(k):
        g = lax.div(k, PIECES)
        slot = jnp.where(g == 0, 1 + p, jnp.where(g == 1, 2 - p, 3))
        return send(piece(slot, m, k), piece(slot, m, k), zs.at[k], zr.at[k], near_z)

    own_rows = pl.ds(core * entries, entries)
    other_rows = pl.ds((1 - core) * entries, entries)
    w_local = pltpu.make_async_copy(head, W.at[own_rows], w_sem.at[0])
    w_send = send(head, W.at[own_rows], w_sem.at[1], w_sem.at[2], near_core)
    w_in = send(head, W.at[other_rows], w_sem.at[1], w_sem.at[2], near_core)
    goals = [
        send(goal, tgt.at[j], gs.at[j - 1], gr.at[j - 1], where)
        for j, where in ((1, near_x), (2, near_y), (3, near_d))
    ]
    stats = [
        send(st.at[j], rs.at[j], ss.at[j - 1], sr.at[j - 1], where)
        for j, where in ((1, near_x), (2, near_y), (3, near_d))
    ]

    for t in (p, q, m):
        load(t).start()
    barrier = pltpu.get_barrier_semaphore()
    for where in partners:
        pl.semaphore_signal(barrier, inc=1, device_id=where, device_id_type=MESH)
    w_local.start()

    def scale_of(t):
        load(t).wait()
        states = raw[t]
        return lax.rsqrt(jnp.mean(states * states, axis=1, keepdims=True) + epsilon)

    def normalise(t, scale, j):
        part = pl.ds(j * size, size)
        T[0, t, part, :] = (raw[t, :, part] * scale * gain[part][None, :]).astype(jnp.bfloat16).T

    scale_p = scale_of(p)
    normalise(p, scale_p, 0)
    pl.semaphore_wait(barrier, len(partners))
    Y(0).start()
    w_send.start()
    scale_q = scale_of(q)
    normalise(q, scale_q, 0)
    X(0).start()
    for k in range(1, WINDOW):
        normalise(p, scale_p, k)
        Y(k).start()
        normalise(q, scale_q, k)
        X(k).start()
    for copy in goals:
        copy.start()
    for k in range(WINDOW, PIECES):
        normalise(p, scale_p, k)
        normalise(q, scale_q, k)
    scale_m = scale_of(m)
    for k in range(PIECES):
        normalise(m, scale_m, k)
    tgt[0] = goal[...]

    middle = width // 2
    blocks = W.shape[0] // BLOCK

    def begin(u, t):
        for i in range(blocks):
            rows = pl.ds(i * BLOCK, BLOCK)
            begun[u, rows, :] = jnp.dot(
                W[rows, pl.ds(0, middle)], T[3, t, pl.ds(0, middle), :],
                preferred_element_type=jnp.float32,
            )

    def end(u, t):
        def score(i):
            rows = pl.ds(i * BLOCK, BLOCK)
            return begun[u, rows, :] + jnp.dot(
                W[rows, pl.ds(middle, middle)], T[3, t, pl.ds(middle, middle), :],
                preferred_element_type=jnp.float32,
            )

        unit(3, t, score)

    def unit(slot, t, score):
        wanted = tgt[slot, t, 0:1, :] - base
        zero = jnp.zeros((8, third), jnp.float32)
        top, total, tilted, target = jnp.full((8, third), lowest, jnp.float32), zero, zero, zero
        following = score(0)
        for i in range(blocks):
            logits = following
            if i + 1 < blocks:
                following = score(i + 1)
            entry = lax.broadcasted_iota(jnp.int32, logits.shape, 0)
            hit = jnp.where(entry == wanted - i * BLOCK, logits, 0.0)
            target = target + jnp.sum(hit.reshape(BLOCK // 8, 8, third), axis=0)
            logits = logits.reshape(BLOCK // 8, 8, third)
            higher = jnp.maximum(top, jnp.max(logits, axis=0))
            factor = jnp.exp(top - higher)
            weights = jnp.exp(logits - higher[None])
            total = total * factor + jnp.sum(weights, axis=0)
            tilted = tilted * factor + jnp.sum(weights * logits, axis=0)
            top = higher
        highest = jnp.max(top, axis=0, keepdims=True)
        factor = jnp.exp(top - highest)
        st[slot, t] = rows_of(
            (
                highest,
                jnp.sum(total * factor, axis=0, keepdims=True),
                jnp.sum(tilted * factor, axis=0, keepdims=True),
                jnp.sum(target, axis=0, keepdims=True),
            ),
            (8, third),
        )

    def whole(slot, t):
        def score(i):
            return jnp.dot(
                W[pl.ds(i * BLOCK, BLOCK), :], T[slot, t], preferred_element_type=jnp.float32
            )

        unit(slot, t, score)

    def pick(g, u):
        slot = jnp.where(g == 0, 0, 1 + u)
        t = jnp.where(g == 1, q - u, p + u)
        late = jnp.where(g == 1, 1 + p, jnp.where(g == 2, 2 - p, 0))
        return jnp.where(u == 2, late, slot), jnp.where(u == 2, m, t)

    def arrive(first, last):
        def step(k, carry):
            Z_in(k).wait_recv()
            return carry

        lax.fori_loop(first, last, step, 0)

    def wave(k, carry):
        g, u = lax.div(k, PIECES), lax.rem(k, PIECES)
        X(k).wait_recv()

        @pl.when(k + WINDOW < waves)
        def _():
            X(k + WINDOW).start()

        Y(k).wait_recv()

        @pl.when(k + WINDOW < waves)
        def _():
            Y(k + WINDOW).start()

        Z(k).start()

        @pl.when(k == 0)
        def _():
            w_local.wait()
            w_in.wait_recv()
            for copy in goals:
                copy.wait_recv()

        @pl.when((u == 2) & (g > 0))
        def _():
            arrive((g - 1) * PIECES, g * PIECES)

        @pl.when(u < 3)
        def _():
            whole(*pick(g, u))

        return carry

    def first_halves(u, carry):
        begin(u, p + u)
        return carry

    def second_halves(u, carry):
        end(u, p + u)
        return carry

    lax.fori_loop(0, waves - 1, wave, 0)
    lax.fori_loop(0, 2, first_halves, 0)
    wave(waves - 1, 0)
    stats[0].start()
    stats[1].start()
    lax.fori_loop(0, 2, second_halves, 0)
    arrive(2 * PIECES, 2 * PIECES + PIECES // 2)
    begin(2, m)
    arrive(2 * PIECES + PIECES // 2, waves)
    end(2, m)
    stats[2].start()
    for copy in stats:
        copy.wait_recv()
    top, total, tilted, target = merge([st[0], rs[1], rs[2], rs[3]])
    rz[z] = rows_of((top, total, tilted, target), (3, 8, third))

    def V(k, source):
        return send(rz.at[source], rz.at[source], vs.at[k - 1], vr.at[k - 1], far_z[k - 1])

    for k in range(1, nz):
        V(k, z).start()
    for k in range(1, nz):
        V(k, lax.rem(z + nz - k, nz)).wait_recv()
    top, total, tilted, target = merge([rz[i] for i in range(nz)])
    log_total = top + jnp.log(total)
    chosen = target - log_total
    spread = log_total - tilted / total
    for t in range(3):
        slots = pl.ds(t * third, third)
        position = lax.broadcasted_iota(jnp.int32, (1, third), 1) + t * third
        live = position < lengths[0]
        log_probs[slots] = jnp.where(live, chosen[t], 0.0)[0]
        entropies[slots] = jnp.where(live, spread[t], 0.0)[0]

    w_send.wait_send()

    def sent(k, carry):
        X(k).wait_send()
        Y(k).wait_send()
        Z(k).wait_send()
        return carry

    lax.fori_loop(0, waves, sent, 0)
    for copy in goals + stats:
        copy.wait_send()
    for k in range(1, nz):
        V(k, z).wait_send()


def fused(nz, hidden_states, norm_gain, head_weight, target_ids, lengths):
    rows, width = hidden_states.shape
    entries = head_weight.shape[0]
    third = rows // 3
    dma = pltpu.SemaphoreType.DMA
    any_space = pl.BlockSpec(memory_space=pl.ANY)
    vmem = pl.BlockSpec(memory_space=pltpu.VMEM)
    return pl.pallas_call(
        functools.partial(kernel, nz),
        out_shape=(jax.ShapeDtypeStruct((rows,), jnp.float32),) * 2,
        in_specs=[any_space, vmem, any_space, vmem, pl.BlockSpec(memory_space=pltpu.SMEM)],
        out_specs=(vmem, vmem),
        scratch_shapes=[
            pltpu.VMEM((4, 3, width, third), jnp.bfloat16),
            pltpu.VMEM((2 * entries, width), jnp.bfloat16),
            pltpu.VMEM((3, third, width), jnp.float32),
            pltpu.VMEM((3, 2 * entries, third), jnp.float32),
            pltpu.VMEM((3, 8, third), jnp.int32),
            pltpu.VMEM((4, 3, 8, third), jnp.int32),
            pltpu.VMEM((4, 3, 8, third), jnp.float32),
            pltpu.VMEM((4, 3, 8, third), jnp.float32),
            pltpu.VMEM((nz, 3, 8, third), jnp.float32),
            dma((3,)), dma((3,)),
            *[dma((3 * PIECES,)) for _ in range(6)],
            dma((3,)), dma((3,)), dma((3,)), dma((3,)),
            dma((nz - 1,)), dma((nz - 1,)),
        ],
        compiler_params=pltpu.CompilerParams(
            collective_id=0, has_side_effects=True, vmem_limit_bytes=56 * 1024 * 1024
        ),
        cost_estimate=pl.CostEstimate(
            flops=2 * 4 * rows * 2 * entries * width,
            bytes_accessed=rows * width * 4 + entries * width * 2,
            transcendentals=4 * rows * 2 * entries,
        ),
    )(hidden_states, norm_gain, head_weight, target_ids, lengths)


def gathered(hidden_states, norm_gain, head_weight, target_ids, lengths):
    row_count = hidden_states.shape[0]
    scale = lax.rsqrt(jnp.mean(hidden_states * hidden_states, axis=1, keepdims=True) + epsilon)
    normed = (hidden_states * scale * norm_gain).astype(jnp.bfloat16)
    slice_width = head_weight.shape[0] * lax.axis_size("dp")
    goal_cols = target_ids - lax.axis_index("vocab") * slice_width
    live_mask = jnp.arange(row_count, dtype=jnp.int32) < lengths[0]
    logits = lax.dot_general(
        normed, lax.all_gather(head_weight, "dp", axis=0, tiled=True),
        (((1,), (1,)), ((), ())), preferred_element_type=jnp.float32,
    )
    columns = jnp.arange(logits.shape[1], dtype=jnp.int32)
    highest = jnp.max(logits, axis=1)
    weights = jnp.exp(logits - highest[:, None])
    matched = jnp.where(columns[None, :] == goal_cols[:, None], logits, 0.0)
    maxima = lax.pmax(highest, "vocab")
    factor = jnp.exp(highest - maxima)
    totals, tilted, target_logit = lax.psum(
        (
            jnp.sum(weights, axis=1) * factor,
            jnp.sum(weights * logits, axis=1) * factor,
            jnp.sum(matched, axis=1),
        ),
        "vocab",
    )
    log_total = maxima + jnp.log(totals)
    log_probs = jnp.where(live_mask, target_logit - log_total, 0.0)
    entropies = jnp.where(live_mask, log_total - tilted / totals, 0.0)
    return (log_probs, entropies)


def solution(mesh):
    ndp, nz = mesh.shape["dp"], mesh.shape["vocab"]

    def on_device(*args):
        rows, width = args[0].shape
        entries = args[2].shape[0]
        fits = (
            ndp == 8 and nz % 2 == 0 and rows % 768 == 0 and width % 128 == 0
            and 2 * entries % BLOCK == 0
            and 20 * rows * width + 4 * entries * width < 40 * 1024 * 1024
        )
        return fused(nz, *args) if fits else gathered(*args)

    in_specs = (P("dp", None), P(), P(("vocab", "dp"), None), P("dp"), P("dp"))
    out_specs = (P("dp"), P("dp"))
    return jax.shard_map(
        on_device, mesh=mesh, in_specs=in_specs, out_specs=out_specs, check_vma=False
    )
```

```python
import functools

import jax
import jax.numpy as jnp
from jax import lax
from jax.experimental import pallas as pl
from jax.experimental.pallas import tpu as pltpu
from jax.sharding import PartitionSpec as P

epsilon = 1e-05
lowest = -1e30
MESH = pl.DeviceIdType.MESH
BLOCK = 512
PIECES = 4
WINDOW = 2
FIRST = 0
STRIDE = 1


def merge(parts):
    top = parts[0][:, 0:1, :]
    for part in parts[1:]:
        top = jnp.maximum(top, part[:, 0:1, :])
    total = tilted = target = jnp.zeros_like(top)
    for part in parts:
        factor = jnp.exp(part[:, 0:1, :] - top)
        total = total + part[:, 1:2, :] * factor
        tilted = tilted + part[:, 2:3, :] * factor
        target = target + part[:, 3:4, :]
    return top, total, tilted, target


def rows_of(values, shape):
    axis = len(shape) - 2
    row = lax.broadcasted_iota(jnp.int32, shape, axis)
    tile = jnp.zeros(shape, jnp.float32)
    for i, value in enumerate(values):
        tile = jnp.where(row == i, value, tile)
    return tile


def kernel(nz, hid, gain, head, ids, lengths, log_probs, entropies, T, W, raw, scored, goal, tgt, st, rs, rz,
           hid_sem, w_sem, xs, xr, ys, yr, zs, zr, gs, gr, ss, sr, vs, vr):
    dp = lax.axis_index("dp")
    z = lax.axis_index("vocab")
    core = lax.rem(dp, 2)
    xc = lax.rem(lax.div(dp, 2), 2)
    yc = lax.div(dp, 4)
    p = lax.rem(z, 2)
    q = p + 1
    s = 2 * p
    m = 2 - s
    near_core = (dp + 1 - 2 * core, z)
    near_x = (dp + 2 - 4 * xc, z)
    near_y = (dp + 4 - 8 * yc, z)
    near_d = (dp + 2 - 4 * xc + 4 - 8 * yc, z)
    near_z = (dp, z + 1 - 2 * p)
    far_z = [(dp, lax.rem(z + k, nz)) for k in range(1, nz)]
    partners = [near_core, near_x, near_y, near_d] + far_z

    width, third = T.shape[2:]
    size = width // PIECES
    waves = 3 * PIECES
    entries = head.shape[0]
    base = (z * lax.axis_size("dp") + dp - core) * entries

    for t in range(3):
        goal[t] = jnp.broadcast_to(ids[pl.ds(t * third, third)][None, :], (8, third))

    def load(t):
        return pltpu.make_async_copy(
            hid.at[pl.ds(t * third, third)], raw.at[t], hid_sem.at[t]
        )

    def send(src, dst, send_sem, recv_sem, where):
        return pltpu.make_async_remote_copy(
            src_ref=src, dst_ref=dst, send_sem=send_sem, recv_sem=recv_sem,
            device_id=where, device_id_type=MESH,
        )

    def piece(slot, t, k):
        return T.at[slot, t, pl.ds(lax.rem(k, PIECES) * size, size)]

    def X(k):
        g = lax.div(k, PIECES)
        d, t = lax.div(g, 2), q - lax.div(g + 1, 2)
        return send(piece(2 * d, t, k), piece(1 + 2 * d, t, k), xs.at[k], xr.at[k], near_x)

    def Y(k):
        g = lax.div(k, PIECES)
        d, t = lax.div(g, 2), p + lax.div(g + 1, 2)
        return send(piece(d, t, k), piece(2 + d, t, k), ys.at[k], yr.at[k], near_y)

    def Z(k):
        g = lax.div(k, PIECES)
        slot = jnp.where(g == 0, 2 - p, jnp.where(g == 1, 1 + p, 3))
        return send(piece(slot, s, k), piece(slot, s, k), zs.at[k], zr.at[k], near_z)

    def Z_in(k):
        g = lax.div(k, PIECES)
        slot = jnp.where(g == 0, 1 + p, jnp.where(g == 1, 2 - p, 3))
        return send(piece(slot, m, k), piece(slot, m, k), zs.at[k], zr.at[k], near_z)

    own_rows = pl.ds(core * entries, entries)
    other_rows = pl.ds((1 - core) * entries, entries)
    w_local = pltpu.make_async_copy(head, W.at[own_rows], w_sem.at[0])
    w_send = send(head, W.at[own_rows], w_sem.at[1], w_sem.at[2], near_core)
    w_in = send(head, W.at[other_rows], w_sem.at[1], w_sem.at[2], near_core)
    goals = [
        send(goal, tgt.at[j], gs.at[j - 1], gr.at[j - 1], where)
        for j, where in ((1, near_x), (2, near_y), (3, near_d))
    ]
    stats = [
        send(st.at[j], rs.at[j], ss.at[j - 1], sr.at[j - 1], where)
        for j, where in ((1, near_x), (2, near_y), (3, near_d))
    ]

    for t in (p, q, m):
        load(t).start()
    barrier = pltpu.get_barrier_semaphore()
    for where in partners:
        pl.semaphore_signal(barrier, inc=1, device_id=where, device_id_type=MESH)
    w_local.start()

    def normalise(t):
        load(t).wait()
        states = raw[t]
        scale = lax.rsqrt(jnp.mean(states * states, axis=1, keepdims=True) + epsilon)
        T[0, t] = (states * scale * gain[...][None, :]).astype(jnp.bfloat16).T

    normalise(p)
    pl.semaphore_wait(barrier, len(partners))
    Y(0).start()
    w_send.start()
    normalise(q)
    X(0).start()
    for copy in goals:
        copy.start()
    normalise(m)
    tgt[0] = goal[...]
    for k in range(1, WINDOW):
        Y(k).start()
        X(k).start()

    def unit(slot, t):
        ahead = tgt[slot, t] - base - lax.broadcasted_iota(jnp.int32, (8, third), 0)
        zero = jnp.zeros((8, third), jnp.float32)
        top, total, tilted, target = jnp.full((8, third), lowest, jnp.float32), zero, zero, zero

        def score(i):
            scored[i % 2] = jnp.dot(
                W[pl.ds(i * BLOCK, BLOCK), :], T[slot, t], preferred_element_type=jnp.float32
            )

        blocks = W.shape[0] // BLOCK
        score(0)
        for i in range(blocks):
            if i + 1 < blocks:
                score(i + 1)
            higher = top
            for r in range(0, BLOCK, 8):
                higher = jnp.maximum(higher, scored[i % 2, pl.ds(r, 8), :])
            factor = jnp.exp(top - higher)
            total, tilted, top = total * factor, tilted * factor, higher
            for r in range(0, BLOCK, 8):
                logits = scored[i % 2, pl.ds(r, 8), :]
                weights = jnp.exp(logits - top)
                total = total + weights
                tilted = tilted + weights * logits
                target = target + jnp.where(ahead == i * BLOCK + r, logits, 0.0)
        highest = jnp.max(top, axis=0, keepdims=True)
        factor = jnp.exp(top - highest)
        st[slot, t] = rows_of(
            (
                highest,
                jnp.sum(total * factor, axis=0, keepdims=True),
                jnp.sum(tilted * factor, axis=0, keepdims=True),
                jnp.sum(target, axis=0, keepdims=True),
            ),
            (8, third),
        )

    def pick(g, u):
        slot = jnp.where(g == 0, 0, jnp.where(g == 3, 3, 1 + u))
        t = jnp.where(g == 1, q - u, p + u)
        late = jnp.where(g == 1, 1 + p, jnp.where(g == 2, 2 - p, g))
        return jnp.where(u == 2, late, slot), jnp.where(u == 2, m, t)

    def step(k, carry):
        g, j = lax.div(k, PIECES), lax.rem(k, PIECES)
        tail = k >= waves
        u = jnp.where(tail, j, lax.div(j - FIRST, STRIDE))
        turn = tail | ((j >= FIRST) & (u < 3) & (lax.rem(j - FIRST + PIECES * STRIDE, STRIDE) == 0))

        @pl.when(k < waves)
        def _():
            X(k).wait_recv()

        @pl.when(k + WINDOW < waves)
        def _():
            X(k + WINDOW).start()

        @pl.when(k < waves)
        def _():
            Y(k).wait_recv()

        @pl.when(k + WINDOW < waves)
        def _():
            Y(k + WINDOW).start()

        @pl.when(k < waves)
        def _():
            Z(k).start()

        @pl.when(k == FIRST)
        def _():
            w_local.wait()
            w_in.wait_recv()
            for copy in goals:
                copy.wait_recv()

        @pl.when(k == waves)
        def _():
            stats[0].start()
            stats[1].start()

        @pl.when(turn & (u == 2) & (g > 0))
        def _():
            def arrive(i, carry):
                Z_in((g - 1) * PIECES + i).wait_recv()
                return carry

            lax.fori_loop(0, PIECES, arrive, 0)

        @pl.when(turn)
        def _():
            unit(*pick(g, u))

        return carry

    lax.fori_loop(0, waves + 3, step, 0)
    stats[2].start()
    for copy in stats:
        copy.wait_recv()
    top, total, tilted, target = merge([st[0], rs[1], rs[2], rs[3]])
    rz[z] = rows_of((top, total, tilted, target), (3, 8, third))

    def V(k, source):
        return send(rz.at[source], rz.at[source], vs.at[k - 1], vr.at[k - 1], far_z[k - 1])

    for k in range(1, nz):
        V(k, z).start()
    for k in range(1, nz):
        V(k, lax.rem(z + nz - k, nz)).wait_recv()
    top, total, tilted, target = merge([rz[i] for i in range(nz)])
    log_total = top + jnp.log(total)
    chosen = target - log_total
    spread = log_total - tilted / total
    for t in range(3):
        slots = pl.ds(t * third, third)
        position = lax.broadcasted_iota(jnp.int32, (1, third), 1) + t * third
        live = position < lengths[0]
        log_probs[slots] = jnp.where(live, chosen[t], 0.0)[0]
        entropies[slots] = jnp.where(live, spread[t], 0.0)[0]

    w_send.wait_send()

    def sent(k, carry):
        X(k).wait_send()
        Y(k).wait_send()
        Z(k).wait_send()
        return carry

    lax.fori_loop(0, waves, sent, 0)
    for copy in goals + stats:
        copy.wait_send()
    for k in range(1, nz):
        V(k, z).wait_send()


def fused(nz, hidden_states, norm_gain, head_weight, target_ids, lengths):
    rows, width = hidden_states.shape
    entries = head_weight.shape[0]
    third = rows // 3
    dma = pltpu.SemaphoreType.DMA
    any_space = pl.BlockSpec(memory_space=pl.ANY)
    vmem = pl.BlockSpec(memory_space=pltpu.VMEM)
    return pl.pallas_call(
        functools.partial(kernel, nz),
        out_shape=(jax.ShapeDtypeStruct((rows,), jnp.float32),) * 2,
        in_specs=[any_space, vmem, any_space, vmem, pl.BlockSpec(memory_space=pltpu.SMEM)],
        out_specs=(vmem, vmem),
        scratch_shapes=[
            pltpu.VMEM((4, 3, width, third), jnp.bfloat16),
            pltpu.VMEM((2 * entries, width), jnp.bfloat16),
            pltpu.VMEM((3, third, width), jnp.float32),
            pltpu.VMEM((2, BLOCK, third), jnp.float32),
            pltpu.VMEM((3, 8, third), jnp.int32),
            pltpu.VMEM((4, 3, 8, third), jnp.int32),
            pltpu.VMEM((4, 3, 8, third), jnp.float32),
            pltpu.VMEM((4, 3, 8, third), jnp.float32),
            pltpu.VMEM((nz, 3, 8, third), jnp.float32),
            dma((3,)), dma((3,)),
            *[dma((3 * PIECES,)) for _ in range(6)],
            dma((3,)), dma((3,)), dma((3,)), dma((3,)),
            dma((nz - 1,)), dma((nz - 1,)),
        ],
        compiler_params=pltpu.CompilerParams(
            collective_id=0, has_side_effects=True, vmem_limit_bytes=56 * 1024 * 1024
        ),
        cost_estimate=pl.CostEstimate(
            flops=2 * 4 * rows * 2 * entries * width,
            bytes_accessed=rows * width * 4 + entries * width * 2,
            transcendentals=4 * rows * 2 * entries,
        ),
    )(hidden_states, norm_gain, head_weight, target_ids, lengths)


def gathered(hidden_states, norm_gain, head_weight, target_ids, lengths):
    row_count = hidden_states.shape[0]
    scale = lax.rsqrt(jnp.mean(hidden_states * hidden_states, axis=1, keepdims=True) + epsilon)
    normed = (hidden_states * scale * norm_gain).astype(jnp.bfloat16)
    slice_width = head_weight.shape[0] * lax.axis_size("dp")
    goal_cols = target_ids - lax.axis_index("vocab") * slice_width
    live_mask = jnp.arange(row_count, dtype=jnp.int32) < lengths[0]
    logits = lax.dot_general(
        normed, lax.all_gather(head_weight, "dp", axis=0, tiled=True),
        (((1,), (1,)), ((), ())), preferred_element_type=jnp.float32,
    )
    columns = jnp.arange(logits.shape[1], dtype=jnp.int32)
    highest = jnp.max(logits, axis=1)
    weights = jnp.exp(logits - highest[:, None])
    matched = jnp.where(columns[None, :] == goal_cols[:, None], logits, 0.0)
    maxima = lax.pmax(highest, "vocab")
    factor = jnp.exp(highest - maxima)
    totals, tilted, target_logit = lax.psum(
        (
            jnp.sum(weights, axis=1) * factor,
            jnp.sum(weights * logits, axis=1) * factor,
            jnp.sum(matched, axis=1),
        ),
        "vocab",
    )
    log_total = maxima + jnp.log(totals)
    log_probs = jnp.where(live_mask, target_logit - log_total, 0.0)
    entropies = jnp.where(live_mask, log_total - tilted / totals, 0.0)
    return (log_probs, entropies)


def solution(mesh):
    ndp, nz = mesh.shape["dp"], mesh.shape["vocab"]

    def on_device(*args):
        rows, width = args[0].shape
        entries = args[2].shape[0]
        fits = (
            ndp == 8 and nz % 2 == 0 and rows % 768 == 0 and width % 128 == 0
            and 2 * entries % BLOCK == 0
            and 20 * rows * width + 4 * entries * width < 40 * 1024 * 1024
        )
        return fused(nz, *args) if fits else gathered(*args)

    in_specs = (P("dp", None), P(), P(("vocab", "dp"), None), P("dp"), P("dp"))
    out_specs = (P("dp"), P("dp"))
    return jax.shard_map(
        on_device, mesh=mesh, in_specs=in_specs, out_specs=out_specs, check_vma=False
    )
```

```python
import functools

import jax
import jax.numpy as jnp
from jax import lax
from jax.experimental import pallas as pl
from jax.experimental.pallas import tpu as pltpu
from jax.sharding import PartitionSpec as P

epsilon = 1e-05
lowest = -1e30
MESH = pl.DeviceIdType.MESH
BLOCK = 512
PIECES = 4
WINDOW = 3
FIRST = 0
STRIDE = 1


def merge(parts):
    top = parts[0][:, 0:1, :]
    for part in parts[1:]:
        top = jnp.maximum(top, part[:, 0:1, :])
    total = tilted = target = jnp.zeros_like(top)
    for part in parts:
        factor = jnp.exp(part[:, 0:1, :] - top)
        total = total + part[:, 1:2, :] * factor
        tilted = tilted + part[:, 2:3, :] * factor
        target = target + part[:, 3:4, :]
    return top, total, tilted, target


def rows_of(values, shape):
    axis = len(shape) - 2
    row = lax.broadcasted_iota(jnp.int32, shape, axis)
    tile = jnp.zeros(shape, jnp.float32)
    for i, value in enumerate(values):
        tile = jnp.where(row == i, value, tile)
    return tile


def kernel(nz, hid, gain, head, ids, lengths, log_probs, entropies, T, W, raw, scored, goal, tgt, st, rs, rz,
           hid_sem, w_sem, xs, xr, ys, yr, zs, zr, gs, gr, ss, sr, vs, vr):
    dp = lax.axis_index("dp")
    z = lax.axis_index("vocab")
    core = lax.rem(dp, 2)
    xc = lax.rem(lax.div(dp, 2), 2)
    yc = lax.div(dp, 4)
    p = lax.rem(z, 2)
    q = p + 1
    s = 2 * p
    m = 2 - s
    near_core = (dp + 1 - 2 * core, z)
    near_x = (dp + 2 - 4 * xc, z)
    near_y = (dp + 4 - 8 * yc, z)
    near_d = (dp + 2 - 4 * xc + 4 - 8 * yc, z)
    near_z = (dp, z + 1 - 2 * p)
    far_z = [(dp, lax.rem(z + k, nz)) for k in range(1, nz)]
    partners = [near_core, near_x, near_y, near_d] + far_z

    width, third = T.shape[2:]
    size = width // PIECES
    waves = 3 * PIECES
    entries = head.shape[0]
    base = (z * lax.axis_size("dp") + dp - core) * entries

    for t in range(3):
        goal[t] = jnp.broadcast_to(ids[pl.ds(t * third, third)][None, :], (8, third))

    def load(t):
        return pltpu.make_async_copy(
            hid.at[pl.ds(t * third, third)], raw.at[t], hid_sem.at[t]
        )

    def send(src, dst, send_sem, recv_sem, where):
        return pltpu.make_async_remote_copy(
            src_ref=src, dst_ref=dst, send_sem=send_sem, recv_sem=recv_sem,
            device_id=where, device_id_type=MESH,
        )

    def piece(slot, t, k):
        return T.at[slot, t, pl.ds(lax.rem(k, PIECES) * size, size)]

    def X(k):
        g = lax.div(k, PIECES)
        d, t = lax.div(g, 2), q - lax.div(g + 1, 2)
        return send(piece(2 * d, t, k), piece(1 + 2 * d, t, k), xs.at[k], xr.at[k], near_x)

    def Y(k):
        g = lax.div(k, PIECES)
        d, t = lax.div(g, 2), p + lax.div(g + 1, 2)
        return send(piece(d, t, k), piece(2 + d, t, k), ys.at[k], yr.at[k], near_y)

    def Z(k):
        g = lax.div(k, PIECES)
        slot = jnp.where(g == 0, 2 - p, jnp.where(g == 1, 1 + p, 3))
        return send(piece(slot, s, k), piece(slot, s, k), zs.at[k], zr.at[k], near_z)

    def Z_in(k):
        g = lax.div(k, PIECES)
        slot = jnp.where(g == 0, 1 + p, jnp.where(g == 1, 2 - p, 3))
        return send(piece(slot, m, k), piece(slot, m, k), zs.at[k], zr.at[k], near_z)

    own_rows = pl.ds(core * entries, entries)
    other_rows = pl.ds((1 - core) * entries, entries)
    w_local = pltpu.make_async_copy(head, W.at[own_rows], w_sem.at[0])
    w_send = send(head, W.at[own_rows], w_sem.at[1], w_sem.at[2], near_core)
    w_in = send(head, W.at[other_rows], w_sem.at[1], w_sem.at[2], near_core)
    goals = [
        send(goal, tgt.at[j], gs.at[j - 1], gr.at[j - 1], where)
        for j, where in ((1, near_x), (2, near_y), (3, near_d))
    ]
    stats = [
        send(st.at[j], rs.at[j], ss.at[j - 1], sr.at[j - 1], where)
        for j, where in ((1, near_x), (2, near_y), (3, near_d))
    ]

    for t in (p, q, m):
        load(t).start()
    barrier = pltpu.get_barrier_semaphore()
    for where in partners:
        pl.semaphore_signal(barrier, inc=1, device_id=where, device_id_type=MESH)
    w_local.start()

    def normalise(t):
        load(t).wait()
        states = raw[t]
        scale = lax.rsqrt(jnp.mean(states * states, axis=1, keepdims=True) + epsilon)
        T[0, t] = (states * scale * gain[...][None, :]).astype(jnp.bfloat16).T

    normalise(p)
    pl.semaphore_wait(barrier, len(partners))
    Y(0).start()
    w_send.start()
    normalise(q)
    X(0).start()
    for copy in goals:
        copy.start()
    normalise(m)
    tgt[0] = goal[...]
    for k in range(1, WINDOW):
        Y(k).start()
        X(k).start()

    def unit(slot, t):
        ahead = tgt[slot, t] - base - lax.broadcasted_iota(jnp.int32, (8, third), 0)
        zero = jnp.zeros((8, third), jnp.float32)
        top, total, tilted, target = jnp.full((8, third), lowest, jnp.float32), zero, zero, zero

        def score(i):
            scored[i % 2] = jnp.dot(
                W[pl.ds(i * BLOCK, BLOCK), :], T[slot, t], preferred_element_type=jnp.float32
            )

        blocks = W.shape[0] // BLOCK
        score(0)
        for i in range(blocks):
            if i + 1 < blocks:
                score(i + 1)
            higher = top
            for r in range(0, BLOCK, 8):
                higher = jnp.maximum(higher, scored[i % 2, pl.ds(r, 8), :])
            factor = jnp.exp(top - higher)
            total, tilted, top = total * factor, tilted * factor, higher
            for r in range(0, BLOCK, 8):
                logits = scored[i % 2, pl.ds(r, 8), :]
                weights = jnp.exp(logits - top)
                total = total + weights
                tilted = tilted + weights * logits
                target = target + jnp.where(ahead == i * BLOCK + r, logits, 0.0)
        highest = jnp.max(top, axis=0, keepdims=True)
        factor = jnp.exp(top - highest)
        st[slot, t] = rows_of(
            (
                highest,
                jnp.sum(total * factor, axis=0, keepdims=True),
                jnp.sum(tilted * factor, axis=0, keepdims=True),
                jnp.sum(target, axis=0, keepdims=True),
            ),
            (8, third),
        )

    def pick(g, u):
        slot = jnp.where(g == 0, 0, jnp.where(g == 3, 3, 1 + u))
        t = jnp.where(g == 1, q - u, p + u)
        late = jnp.where(g == 1, 1 + p, jnp.where(g == 2, 2 - p, g))
        return jnp.where(u == 2, late, slot), jnp.where(u == 2, m, t)

    def step(k, carry):
        g, j = lax.div(k, PIECES), lax.rem(k, PIECES)
        tail = k >= waves
        u = jnp.where(tail, j, lax.div(j - FIRST, STRIDE))
        turn = tail | ((j >= FIRST) & (u < 3) & (lax.rem(j - FIRST + PIECES * STRIDE, STRIDE) == 0))

        @pl.when(k < waves)
        def _():
            X(k).wait_recv()

        @pl.when(k + WINDOW < waves)
        def _():
            X(k + WINDOW).start()

        @pl.when(k < waves)
        def _():
            Y(k).wait_recv()

        @pl.when(k + WINDOW < waves)
        def _():
            Y(k + WINDOW).start()

        @pl.when(k < waves)
        def _():
            Z(k).start()

        @pl.when(k == FIRST)
        def _():
            w_local.wait()
            w_in.wait_recv()
            for copy in goals:
                copy.wait_recv()

        @pl.when(k == waves)
        def _():
            stats[0].start()
            stats[1].start()

        @pl.when(turn & (u == 2) & (g > 0))
        def _():
            def arrive(i, carry):
                Z_in((g - 1) * PIECES + i).wait_recv()
                return carry

            lax.fori_loop(0, PIECES, arrive, 0)

        @pl.when(turn)
        def _():
            unit(*pick(g, u))

        return carry

    lax.fori_loop(0, waves + 3, step, 0)
    stats[2].start()
    for copy in stats:
        copy.wait_recv()
    top, total, tilted, target = merge([st[0], rs[1], rs[2], rs[3]])
    rz[z] = rows_of((top, total, tilted, target), (3, 8, third))

    def V(k, source):
        return send(rz.at[source], rz.at[source], vs.at[k - 1], vr.at[k - 1], far_z[k - 1])

    for k in range(1, nz):
        V(k, z).start()
    for k in range(1, nz):
        V(k, lax.rem(z + nz - k, nz)).wait_recv()
    top, total, tilted, target = merge([rz[i] for i in range(nz)])
    log_total = top + jnp.log(total)
    chosen = target - log_total
    spread = log_total - tilted / total
    for t in range(3):
        slots = pl.ds(t * third, third)
        position = lax.broadcasted_iota(jnp.int32, (1, third), 1) + t * third
        live = position < lengths[0]
        log_probs[slots] = jnp.where(live, chosen[t], 0.0)[0]
        entropies[slots] = jnp.where(live, spread[t], 0.0)[0]

    w_send.wait_send()

    def sent(k, carry):
        X(k).wait_send()
        Y(k).wait_send()
        Z(k).wait_send()
        return carry

    lax.fori_loop(0, waves, sent, 0)
    for copy in goals + stats:
        copy.wait_send()
    for k in range(1, nz):
        V(k, z).wait_send()


def fused(nz, hidden_states, norm_gain, head_weight, target_ids, lengths):
    rows, width = hidden_states.shape
    entries = head_weight.shape[0]
    third = rows // 3
    dma = pltpu.SemaphoreType.DMA
    any_space = pl.BlockSpec(memory_space=pl.ANY)
    vmem = pl.BlockSpec(memory_space=pltpu.VMEM)
    return pl.pallas_call(
        functools.partial(kernel, nz),
        out_shape=(jax.ShapeDtypeStruct((rows,), jnp.float32),) * 2,
        in_specs=[any_space, vmem, any_space, vmem, pl.BlockSpec(memory_space=pltpu.SMEM)],
        out_specs=(vmem, vmem),
        scratch_shapes=[
            pltpu.VMEM((4, 3, width, third), jnp.bfloat16),
            pltpu.VMEM((2 * entries, width), jnp.bfloat16),
            pltpu.VMEM((3, third, width), jnp.float32),
            pltpu.VMEM((2, BLOCK, third), jnp.float32),
            pltpu.VMEM((3, 8, third), jnp.int32),
            pltpu.VMEM((4, 3, 8, third), jnp.int32),
            pltpu.VMEM((4, 3, 8, third), jnp.float32),
            pltpu.VMEM((4, 3, 8, third), jnp.float32),
            pltpu.VMEM((nz, 3, 8, third), jnp.float32),
            dma((3,)), dma((3,)),
            *[dma((3 * PIECES,)) for _ in range(6)],
            dma((3,)), dma((3,)), dma((3,)), dma((3,)),
            dma((nz - 1,)), dma((nz - 1,)),
        ],
        compiler_params=pltpu.CompilerParams(
            collective_id=0, has_side_effects=True, vmem_limit_bytes=56 * 1024 * 1024
        ),
        cost_estimate=pl.CostEstimate(
            flops=2 * 4 * rows * 2 * entries * width,
            bytes_accessed=rows * width * 4 + entries * width * 2,
            transcendentals=4 * rows * 2 * entries,
        ),
    )(hidden_states, norm_gain, head_weight, target_ids, lengths)


def gathered(hidden_states, norm_gain, head_weight, target_ids, lengths):
    row_count = hidden_states.shape[0]
    scale = lax.rsqrt(jnp.mean(hidden_states * hidden_states, axis=1, keepdims=True) + epsilon)
    normed = (hidden_states * scale * norm_gain).astype(jnp.bfloat16)
    slice_width = head_weight.shape[0] * lax.axis_size("dp")
    goal_cols = target_ids - lax.axis_index("vocab") * slice_width
    live_mask = jnp.arange(row_count, dtype=jnp.int32) < lengths[0]
    logits = lax.dot_general(
        normed, lax.all_gather(head_weight, "dp", axis=0, tiled=True),
        (((1,), (1,)), ((), ())), preferred_element_type=jnp.float32,
    )
    columns = jnp.arange(logits.shape[1], dtype=jnp.int32)
    highest = jnp.max(logits, axis=1)
    weights = jnp.exp(logits - highest[:, None])
    matched = jnp.where(columns[None, :] == goal_cols[:, None], logits, 0.0)
    maxima = lax.pmax(highest, "vocab")
    factor = jnp.exp(highest - maxima)
    totals, tilted, target_logit = lax.psum(
        (
            jnp.sum(weights, axis=1) * factor,
            jnp.sum(weights * logits, axis=1) * factor,
            jnp.sum(matched, axis=1),
        ),
        "vocab",
    )
    log_total = maxima + jnp.log(totals)
    log_probs = jnp.where(live_mask, target_logit - log_total, 0.0)
    entropies = jnp.where(live_mask, log_total - tilted / totals, 0.0)
    return (log_probs, entropies)


def solution(mesh):
    ndp, nz = mesh.shape["dp"], mesh.shape["vocab"]

    def on_device(*args):
        rows, width = args[0].shape
        entries = args[2].shape[0]
        fits = (
            ndp == 8 and nz % 2 == 0 and rows % 768 == 0 and width % 128 == 0
            and 2 * entries % BLOCK == 0
            and 20 * rows * width + 4 * entries * width < 40 * 1024 * 1024
        )
        return fused(nz, *args) if fits else gathered(*args)

    in_specs = (P("dp", None), P(), P(("vocab", "dp"), None), P("dp"), P("dp"))
    out_specs = (P("dp"), P("dp"))
    return jax.shard_map(
        on_device, mesh=mesh, in_specs=in_specs, out_specs=out_specs, check_vma=False
    )
```
